128 devices in a mesh: ctx: 32 (over y, x, core), head: 4 (over z), rep: 1.
Axes of the slice: x: 4, y: 4, z: 4, core: 2. Of those that a mesh axis runs over, the one named last changes fastest.
Arguments:
- queries: bfloat16 [32768, 4096], P(('rep', 'ctx'), 'head'), may hold values from -6 to 6
- keys: bfloat16 [32768, 512], P(('rep', 'ctx'), 'head'), may hold values from -6 to 6
- values: bfloat16 [32768, 512], P(('rep', 'ctx'), 'head'), may hold values from -6 to 6
- grad_out: bfloat16 [32768, 4096], P(('rep', 'ctx'), 'head'), may hold values from -48 to 48
- ancestor_ids: int32 [256, 6], P(('rep', 'ctx')), may hold values from 0 to 255, as said below
- ancestor_count: int32 [256], P(('rep', 'ctx')), may hold values from 0 to 6, as said below
Outputs:
- grad_queries: bfloat16 [32768, 4096], P(('rep', 'ctx'), 'head')
- grad_keys: bfloat16 [32768, 512], P(('rep', 'ctx'), 'head')
- grad_values: bfloat16 [32768, 512], P(('rep', 'ctx'), 'head')
The draws below stay inside these ranges and needn't reach their ends.
Inputs may be any that keep to these rules, and one draw needn't show every extreme that they name: The blocks are the nodes of a tree in depth-first order: block 0 is the root, and the parent of every other block b is block b - 1 or one of its ancestors. For j below ancestor_count[b], ancestor_ids[b, j] is the ancestor of block b at depth j (the root first, then ever deeper); entries past the count are 0. ancestor_count[b] is the depth of block b; some block has 6 ancestors.
All inputs are finite; a program needn't handle non-finite values.
Results may differ from the reference program's by a relative error of at most 0.0052.
Values may be sent and summed in bfloat16 or wider, within the bound.
No kernel may reach another device: no remote copies, remote signals or barrier semaphores. Data moves between devices by JAX's collectives and lax.ppermute only.
A program may use at most 256 MiB of HBM per device.

```python
import jax
import jax.numpy as jnp
from jax import lax

HD = 128
HQ_KV = 8
BLK = 128
MAXA = 6
KV_HEADS = 4
QH = 32
NBLK = 256
TOKENS = 32768


def draw_queries(key, part):
    base_key = jax.random.fold_in(key, 1)
    drawn = jnp.clip(jax.random.normal(base_key, (TOKENS, QH, HD)), -6.0, 6.0)
    return drawn.reshape(TOKENS, QH * HD).astype(jnp.bfloat16)


def draw_keys(key, part):
    base_key = jax.random.fold_in(key, 3)
    drawn = jnp.clip(jax.random.normal(base_key, (TOKENS, KV_HEADS, HD)), -6.0, 6.0)
    return drawn.reshape(TOKENS, KV_HEADS * HD).astype(jnp.bfloat16)


def ancestry(key):
    base_key = jax.random.fold_in(key, 53)
    start_key, pick_key, deep_key, pivot_key = jax.random.split(base_key, 4)
    chain_start = jax.random.randint(start_key, (), 0, NBLK - MAXA)
    pivot_block = jax.random.randint(pivot_key, (), 2, max(3, NBLK // 2))
    pick_values = jax.random.randint(pick_key, (NBLK,), 0, 1 << 20)
    deep_values = jax.random.randint(deep_key, (NBLK,), 0, 3)

    def advance(carry, packed):
        depth_prev, path_ids = carry
        block_index, pick_value, deep_value = packed
        ceiling = jnp.minimum(depth_prev + 1, MAXA)
        forced = (block_index > chain_start) & (block_index <= chain_start + MAXA)
        depth_free = jnp.where(deep_value == 0, ceiling, 1 + pick_value % ceiling)
        depth_late = jnp.where(block_index > pivot_block, jnp.maximum(depth_free, jnp.minimum(3, ceiling)), depth_free)
        depth_pivot = jnp.where(block_index == pivot_block, jnp.minimum(2, ceiling), depth_late)
        depth_now = jnp.where(forced, ceiling, depth_pivot).astype(jnp.int32)
        listed = jnp.where(jnp.arange(MAXA, dtype=jnp.int32) < depth_now, path_ids[:MAXA], 0)
        path_ids = path_ids.at[depth_now].set(block_index)
        return ((depth_now, path_ids), (listed, depth_now))
    initial = (jnp.int32(0), jnp.zeros((MAXA + 1,), jnp.int32))
    block_range = jnp.arange(1, NBLK, dtype=jnp.int32)
    unused, outputs = lax.scan(advance, initial, (block_range, pick_values[1:], deep_values[1:]))
    listed, depths = outputs
    id_rows = jnp.concatenate([jnp.zeros((1, MAXA), jnp.int32), listed], axis=0)
    depth_rows = jnp.concatenate([jnp.zeros((1,), jnp.int32), depths], axis=0)
    return (id_rows, depth_rows)


def draw_ancestor_ids(key, part):
    return ancestry(key)[0]


def draw_ancestor_count(key, part):
    return ancestry(key)[1]


def levels(key, extent, cuts, low, high):
    loudness = 1.0
    for position, parts in cuts:
        heights = jax.random.uniform(jax.random.fold_in(jax.random.fold_in(key, 6), position), (parts,), jnp.float32, low / len(cuts), high / len(cuts))
        loudness = loudness * jnp.repeat(jnp.exp(heights), extent[position] // parts).reshape((-1,) + (1,) * (len(extent) - 1 - position))
    return loudness


def normal_values(own_key, shape, scale, most, cuts=(), kind=jnp.bfloat16):
    gain = levels(own_key, shape, cuts, -0.22, 0.18) if cuts else 1.0
    array = jax.random.normal(own_key, shape, jnp.float32) * scale * gain
    return jnp.minimum(jnp.maximum(array, -most), most).astype(kind)


def setup_inputs(seed: int = 0, part: int = 0) -> dict:
    streams_of = jax.random.split(jax.random.key(seed), 7)
    part_splits = jax.random.split(jax.random.fold_in(streams_of[6], part), 7)
    queries = draw_queries(jax.random.fold_in(jax.random.fold_in(streams_of[6], part), 71), part)
    keys = draw_keys(jax.random.fold_in(jax.random.fold_in(streams_of[6], part), 71), part)
    values = normal_values(part_splits[2], (TOKENS, KV_HEADS * HD), 1.0, 6.0, ((0, 32), (1, 4)))
    grad_out = normal_values(part_splits[3], (TOKENS, QH * HD), 8.0, 48.0, ((0, 32), (1, 4)))
    ancestor_ids = draw_ancestor_ids(jax.random.fold_in(jax.random.fold_in(streams_of[6], part), 71), part)
    ancestor_count = draw_ancestor_count(jax.random.fold_in(jax.random.fold_in(streams_of[6], part), 71), part)
    return {"queries": queries, "keys": keys, "values": values, "grad_out": grad_out, "ancestor_ids": ancestor_ids, "ancestor_count": ancestor_count}


def tile_mask(is_live):
    inner_pos = jnp.arange(BLK, dtype=jnp.int32)
    causal = inner_pos[:, None] >= inner_pos[None, :]
    diagonal = jnp.arange(MAXA + 1, dtype=jnp.int32)[None, :, None] == MAXA
    allowed = jnp.where(diagonal, causal[:, None, :], is_live[None, :, None])
    return allowed.reshape(BLK, (MAXA + 1) * BLK)


def tile_grads(query_tile, grad_tile, key_rows, value_rows, allowed):
    score_scale = HD ** -0.5
    scores = jnp.einsum("qhd,kd->hqk", query_tile, key_rows) * score_scale
    masked = jnp.where(allowed[None], scores, -jnp.inf)
    row_max = jnp.max(masked, axis=-1, keepdims=True)
    row_total = jnp.sum(jnp.where(allowed[None], jnp.exp(scores - row_max), 0.0), axis=-1, keepdims=True)
    log_total = row_max + jnp.log(row_total)
    weights = jnp.where(allowed[None], jnp.exp(scores - log_total), 0.0)
    dprobs = jnp.einsum("qhd,kd->hqk", grad_tile, value_rows)
    row_delta = jnp.sum(weights * dprobs, axis=-1, keepdims=True)
    dscores = weights * (dprobs - row_delta)
    probs_low = lax.optimization_barrier(weights.astype(jnp.bfloat16)).astype(jnp.float32)
    dscores_low = lax.optimization_barrier(dscores.astype(jnp.bfloat16)).astype(jnp.float32)
    grad_query = jnp.einsum("hqk,kd->qhd", dscores_low, key_rows) * score_scale
    grad_key = jnp.einsum("hqk,qhd->kd", dscores_low, query_tile)
    grad_value = jnp.einsum("hqk,qhd->kd", probs_low, grad_tile)
    return grad_query, grad_key, grad_value


def reference(queries, keys, values, grad_out, ancestor_ids, ancestor_count):
    score_scale = HD ** -0.5
    block_ids = jnp.arange(NBLK, dtype=jnp.int32)
    slot_ids = jnp.concatenate([ancestor_ids.astype(jnp.int32), block_ids[:, None]], axis=1)
    slot_pos = jnp.arange(MAXA + 1, dtype=jnp.int32)[None, :]
    slot_live = (slot_pos < ancestor_count.astype(jnp.int32)[:, None]) | (slot_pos == MAXA)
    query_heads = jnp.transpose(queries.astype(jnp.float32).reshape(NBLK, BLK, KV_HEADS, HQ_KV, HD), (2, 0, 1, 3, 4))
    grad_heads = jnp.transpose(grad_out.astype(jnp.float32).reshape(NBLK, BLK, KV_HEADS, HQ_KV, HD), (2, 0, 1, 3, 4))
    key_heads = jnp.transpose(keys.astype(jnp.float32).reshape(NBLK, BLK, KV_HEADS, HD), (2, 0, 1, 3))
    value_heads = jnp.transpose(values.astype(jnp.float32).reshape(NBLK, BLK, KV_HEADS, HD), (2, 0, 1, 3))

    def one_group(packed):
        query_group, grad_group, key_group, value_group = packed

        def one_tile(query_tile, grad_tile, slots, is_live):
            key_rows = key_group[slots].reshape((MAXA + 1) * BLK, HD)
            value_rows = value_group[slots].reshape((MAXA + 1) * BLK, HD)
            return tile_grads(query_tile, grad_tile, key_rows, value_rows, tile_mask(is_live))

        grad_query, grad_key, grad_value = jax.vmap(one_tile)(query_group, grad_group, slot_ids, slot_live)
        flat_ids = slot_ids.reshape(-1)
        key_sums = jnp.zeros((NBLK, BLK, HD), jnp.float32).at[flat_ids].add(grad_key.reshape(-1, BLK, HD))
        value_sums = jnp.zeros((NBLK, BLK, HD), jnp.float32).at[flat_ids].add(grad_value.reshape(-1, BLK, HD))
        return grad_query, key_sums, value_sums

    grad_query, key_sums, value_sums = lax.map(one_group, (query_heads, grad_heads, key_heads, value_heads))
    grad_queries = jnp.transpose(grad_query, (1, 2, 0, 3, 4)).reshape(TOKENS, QH * HD).astype(jnp.bfloat16)
    grad_keys = (jnp.transpose(key_sums, (1, 2, 0, 3)).reshape(TOKENS, KV_HEADS * HD) * score_scale).astype(jnp.bfloat16)
    grad_values = jnp.transpose(value_sums, (1, 2, 0, 3)).reshape(TOKENS, KV_HEADS * HD).astype(jnp.bfloat16)
    return (grad_queries, grad_keys, grad_values)
```

```python
import functools

import jax
import jax.numpy as jnp
from jax import lax
from jax.experimental import pallas as pl
from jax.experimental.pallas import tpu as pltpu
from jax.sharding import PartitionSpec as P

HD = 128
HQ = 8
BLK = 128
MAXA = 6
OWN = 8
SHARDS = 32
ROWS = HQ * BLK
CHUNK = 256
PIECE = 8 * MAXA
MARK = 1e30
MARK_MIN = 1e29
SCALE = HD ** (-0.5)
LOG2E = 1.4426950408889634
MIB = 1024 * 1024

F32 = jnp.float32
BF16 = jnp.bfloat16


def last_of_depth(count_ref, depth):
    found = jnp.int32(-1)
    for b in range(OWN):
        found = jnp.where(count_ref[b] == depth, jnp.int32(b), found)
    return found


def pack_kernel(count_ref, k_ref, v_ref, out_ref):
    for half, ref in enumerate((k_ref, v_ref)):
        parts = []
        for j in range(MAXA):
            last = last_of_depth(count_ref, j)
            row = pl.multiple_of(jnp.maximum(last, 0) * BLK, BLK)
            block = ref[pl.ds(row, BLK), :].astype(F32)
            block = jnp.where(last >= 0, block, MARK)
            parts.append(block.reshape(16, 8, HD))
        out_ref[pl.ds(half * 16, 16)] = jnp.concatenate(parts, axis=1).astype(BF16)


def pack(keys, values, count):
    return pl.pallas_call(
        pack_kernel,
        out_shape=jax.ShapeDtypeStruct((SHARDS, PIECE, HD), BF16),
        in_specs=[
            pl.BlockSpec(memory_space=pltpu.SMEM),
            pl.BlockSpec(memory_space=pltpu.VMEM),
            pl.BlockSpec(memory_space=pltpu.VMEM),
        ],
        out_specs=pl.BlockSpec(memory_space=pltpu.VMEM),
        name="pack",
    )(count, keys, values)


def stack_kernel(in_ref, out_ref):
    held = jnp.full((PIECE, HD), MARK, F32)
    for t in range(SHARDS):
        out_ref[t] = held.astype(BF16)
        x = in_ref[t].astype(F32)
        held = jnp.where(x < MARK_MIN, x, held)


def stack(pieces):
    return pl.pallas_call(
        stack_kernel,
        out_shape=jax.ShapeDtypeStruct((SHARDS, PIECE, HD), BF16),
        in_specs=[pl.BlockSpec(memory_space=pltpu.VMEM)],
        out_specs=pl.BlockSpec(memory_space=pltpu.VMEM),
        name="stack",
    )(pieces)


def segsum_kernel(flag_ref, in_ref, out_ref):
    total = jnp.zeros((PIECE, HD), F32)
    for t in range(SHARDS - 1, -1, -1):
        here = flag_ref[t].astype(F32) < MARK_MIN
        out_ref[t] = jnp.where(here, total, 0.0).astype(BF16)
        total = jnp.where(here, 0.0, total) + in_ref[t].astype(F32)


def segsum(flags, pieces):
    return pl.pallas_call(
        segsum_kernel,
        out_shape=jax.ShapeDtypeStruct((SHARDS, PIECE, HD), BF16),
        in_specs=[pl.BlockSpec(memory_space=pltpu.VMEM)] * 2,
        out_specs=pl.BlockSpec(memory_space=pltpu.VMEM),
        name="segsum",
    )(flags, pieces)


def final_kernel(count_ref, dk_ref, dv_ref, in_ref, gk_ref, gv_ref, acc):
    for half, (ref, out, scale) in enumerate(((dk_ref, gk_ref, SCALE), (dv_ref, gv_ref, 1.0))):
        acc[...] = ref[...]
        piece = in_ref[pl.ds(half * 16, 16)].astype(F32)
        for j in range(MAXA):
            last = last_of_depth(count_ref, j)
            row = pl.multiple_of(jnp.maximum(last, 0) * BLK, BLK)
            term = piece[:, 8 * j : 8 * j + 8, :].reshape(BLK, HD)
            acc[pl.ds(row, BLK), :] += jnp.where(last >= 0, term, 0.0)
        out[...] = (acc[...] * scale).astype(BF16)


def final(count, dk, dv, pieces):
    shape = jax.ShapeDtypeStruct((OWN * BLK, HD), BF16)
    return pl.pallas_call(
        final_kernel,
        out_shape=(shape, shape),
        in_specs=[pl.BlockSpec(memory_space=pltpu.SMEM)] + [pl.BlockSpec(memory_space=pltpu.VMEM)] * 3,
        out_specs=[pl.BlockSpec(memory_space=pltpu.VMEM)] * 2,
        scratch_shapes=[pltpu.VMEM((OWN * BLK, HD), F32)],
        name="final",
    )(count, dk, dv, pieces)


def nt(a, b):
    return lax.dot_general(a, b, (((1,), (1,)), ((), ())), preferred_element_type=F32)


def nn(a, b):
    return lax.dot_general(a, b, (((1,), (0,)), ((), ())), preferred_element_type=F32)


def tn(a, b):
    return lax.dot_general(a, b, (((0,), (0,)), ((), ())), preferred_element_type=F32)


def attn_kernel(
    ids_ref,
    count_ref,
    base_ref,
    q_ref,
    o_ref,
    k_ref,
    v_ref,
    ext_ref,
    dq_ref,
    dk_ref,
    dv_ref,
    back_ref,
    kt,
    vt,
    dke,
    dve,
    qs,
    os,
    e_scr,
    d_scr,
    p_scr,
    s_scr,
    kb,
):
    b = pl.program_id(0)
    base = base_ref[0]

    @pl.when(b == 0)
    def _():
        kt[pl.ds(0, OWN * BLK), :] = k_ref[...]
        vt[pl.ds(0, OWN * BLK), :] = v_ref[...]
        for half, tab in enumerate((kt, vt)):
            piece = ext_ref[pl.ds(half * 16, 16)].astype(F32)
            for j in range(MAXA):
                rows = piece[:, 8 * j : 8 * j + 8, :].reshape(BLK, HD)
                tab[pl.ds((OWN + j) * BLK, BLK), :] = rows.astype(BF16)
        dke[...] = jnp.zeros_like(dke)
        dve[...] = jnp.zeros_like(dve)

    for h in range(HQ):
        qs[pl.ds(h * BLK, BLK), :] = q_ref[:, h * HD : (h + 1) * HD]
        os[pl.ds(h * BLK, BLK), :] = o_ref[:, h * HD : (h + 1) * HD]

    count = count_ref[b]
    coef = SCALE * LOG2E
    key_pos = lax.broadcasted_iota(jnp.int32, (BLK, CHUNK), 0)
    row_pos = lax.rem(lax.broadcasted_iota(jnp.int32, (BLK, CHUNK), 1), BLK)
    causal = key_pos <= row_pos

    def table_row(j):
        ident = ids_ref[b * MAXA + j]
        place = jnp.where(ident >= base, ident - base, OWN + j)
        return pl.multiple_of(place * BLK, BLK)

    for n in range(MAXA + 1):

        @pl.when(count == n)
        def _(n=n):
            places = [table_row(j) for j in range(n)] + [pl.multiple_of(b * BLK, BLK)]
            nk = (n + 1) * BLK
            for j in range(n + 1):
                kb[pl.ds(j * BLK, BLK), :] = kt[pl.ds(places[j], BLK), :]

            def visit(c, carry):
                start = pl.multiple_of(c * CHUNK, CHUNK)
                qc = qs[pl.ds(start, CHUNK), :]
                oc = os[pl.ds(start, CHUNK), :]
                tops, sums, dots = [], [], []
                for j in range(n + 1):
                    s = nt(kt[pl.ds(places[j], BLK), :], qc)
                    if j == n:
                        s = jnp.where(causal, s, -jnp.inf)
                    top = jnp.max(s, axis=0, keepdims=True)
                    e = jnp.exp2((s - top) * coef)
                    d = nt(vt[pl.ds(places[j], BLK), :], oc)
                    tops.append(top)
                    sums.append(jnp.sum(e, axis=0, keepdims=True))
                    dots.append(jnp.sum(e * d, axis=0, keepdims=True))
                    e_scr[pl.ds(j * BLK, BLK), :] = e
                    d_scr[pl.ds(j * BLK, BLK), :] = d
                top = functools.reduce(jnp.maximum, tops)
                factors = [jnp.exp2((t - top) * coef) for t in tops]
                total = sum(f * x for f, x in zip(factors, sums))
                inv = 1.0 / total
                delta = sum(f * x for f, x in zip(factors, dots)) * inv
                for j in range(n + 1):
                    p = e_scr[pl.ds(j * BLK, BLK), :] * (factors[j] * inv)
                    ds = p * (d_scr[pl.ds(j * BLK, BLK), :] - delta)
                    p_scr[pl.ds(j * BLK, BLK), pl.ds(start, CHUNK)] = p.astype(BF16)
                    s_scr[pl.ds(j * BLK, BLK), pl.ds(start, CHUNK)] = ds.astype(BF16)
                return carry

            lax.fori_loop(0, ROWS // CHUNK, visit, 0)
            dv = nn(p_scr[pl.ds(0, nk), :], os[...])
            dk = nn(s_scr[pl.ds(0, nk), :], qs[...])
            for j in range(n + 1):
                dke[pl.ds(places[j], BLK), :] += dk[j * BLK : (j + 1) * BLK]
                dve[pl.ds(places[j], BLK), :] += dv[j * BLK : (j + 1) * BLK]
            dq = tn(s_scr[pl.ds(0, nk), :], kb[pl.ds(0, nk), :]) * SCALE
            for h in range(HQ):
                dq_ref[:, h * HD : (h + 1) * HD] = dq[h * BLK : (h + 1) * BLK].astype(BF16)

    @pl.when(b == OWN - 1)
    def _():
        dk_ref[...] = dke[pl.ds(0, OWN * BLK), :]
        dv_ref[...] = dve[pl.ds(0, OWN * BLK), :]
        for half, acc in enumerate((dke, dve)):
            parts = [acc[pl.ds((OWN + j) * BLK, BLK), :].reshape(16, 8, HD) for j in range(MAXA)]
            back_ref[pl.ds(half * 16, 16)] = jnp.concatenate(parts, axis=1).astype(BF16)


def attention(ids, count, base, queries, grad_out, keys, values, ext):
    whole = lambda shape: pl.BlockSpec(shape, lambda b, *_: (0,) * len(shape))
    tiles = OWN + MAXA
    return pl.pallas_call(
        attn_kernel,
        grid_spec=pltpu.PrefetchScalarGridSpec(
            num_scalar_prefetch=3,
            grid=(OWN,),
            in_specs=[
                pl.BlockSpec((BLK, ROWS), lambda b, *_: (b, 0)),
                pl.BlockSpec((BLK, ROWS), lambda b, *_: (b, 0)),
                whole((OWN * BLK, HD)),
                whole((OWN * BLK, HD)),
                whole((SHARDS, PIECE, HD)),
            ],
            out_specs=[
                pl.BlockSpec((BLK, ROWS), lambda b, *_: (b, 0)),
                whole((OWN * BLK, HD)),
                whole((OWN * BLK, HD)),
                whole((SHARDS, PIECE, HD)),
            ],
            scratch_shapes=[
                pltpu.VMEM((tiles * BLK, HD), BF16),
                pltpu.VMEM((tiles * BLK, HD), BF16),
                pltpu.VMEM((tiles * BLK, HD), F32),
                pltpu.VMEM((tiles * BLK, HD), F32),
                pltpu.VMEM((ROWS, HD), BF16),
                pltpu.VMEM((ROWS, HD), BF16),
                pltpu.VMEM(((MAXA + 1) * BLK, CHUNK), F32),
                pltpu.VMEM(((MAXA + 1) * BLK, CHUNK), F32),
                pltpu.VMEM(((MAXA + 1) * BLK, ROWS), BF16),
                pltpu.VMEM(((MAXA + 1) * BLK, ROWS), BF16),
                pltpu.VMEM(((MAXA + 1) * BLK, HD), BF16),
            ],
        ),
        out_shape=(
            jax.ShapeDtypeStruct((OWN * BLK, ROWS), BF16),
            jax.ShapeDtypeStruct((OWN * BLK, HD), F32),
            jax.ShapeDtypeStruct((OWN * BLK, HD), F32),
            jax.ShapeDtypeStruct((SHARDS, PIECE, HD), BF16),
        ),
        compiler_params=pltpu.CompilerParams(vmem_limit_bytes=48 * MIB),
        name="attention",
    )(ids, count, base, queries, grad_out, keys, values, ext)


def body(queries, keys, values, grad_out, ancestor_ids, ancestor_count):
    base = (lax.axis_index("ctx") * OWN).astype(jnp.int32).reshape(1)
    mine = pack(keys, values, ancestor_count)
    pieces = lax.all_to_all(mine, "ctx", 0, 0, tiled=True)
    ext = lax.all_to_all(stack(pieces), "ctx", 0, 0, tiled=True)
    grad_queries, dk, dv, back = attention(
        ancestor_ids.reshape(-1), ancestor_count, base, queries, grad_out, keys, values, ext
    )
    sums = segsum(pieces, lax.all_to_all(back, "ctx", 0, 0, tiled=True))
    terms = lax.all_to_all(sums, "ctx", 0, 0, tiled=True)
    grad_keys, grad_values = final(ancestor_count, dk, dv, terms)
    return (grad_queries, grad_keys, grad_values)


def solution(mesh):
    rows = P(("rep", "ctx"), "head")
    in_specs = (rows, rows, rows, rows, P(("rep", "ctx"), None), P(("rep", "ctx")))
    return jax.shard_map(
        body, mesh=mesh, in_specs=in_specs, out_specs=(rows, rows, rows), check_vma=False
    )
```

```python
import functools

import jax
import jax.numpy as jnp
from jax import lax
from jax.experimental import pallas as pl
from jax.experimental.pallas import tpu as pltpu
from jax.sharding import PartitionSpec as P

HD = 128
HQ = 8
BLK = 128
MAXA = 6
OWN = 8
SHARDS = 32
ROWS = HQ * BLK
CHUNK = 256
PIECE = 8 * MAXA
MARK = 1e30
MARK_MIN = 1e29
SCALE = HD ** (-0.5)
LOG2E = 1.4426950408889634
MIB = 1024 * 1024

F32 = jnp.float32
BF16 = jnp.bfloat16


def last_of_depth(count_ref, depth):
    found = jnp.int32(-1)
    for b in range(OWN):
        found = jnp.where(count_ref[b] == depth, jnp.int32(b), found)
    return found


def pack_kernel(count_ref, k_ref, v_ref, out_ref):
    for half, ref in enumerate((k_ref, v_ref)):
        parts = []
        for j in range(MAXA):
            last = last_of_depth(count_ref, j)
            row = pl.multiple_of(jnp.maximum(last, 0) * BLK, BLK)
            block = ref[pl.ds(row, BLK), :].astype(F32)
            block = jnp.where(last >= 0, block, MARK)
            parts.append(block.reshape(16, 8, HD))
        out_ref[pl.ds(half * 16, 16)] = jnp.concatenate(parts, axis=1).astype(BF16)


def pack(keys, values, count):
    return pl.pallas_call(
        pack_kernel,
        out_shape=jax.ShapeDtypeStruct((SHARDS, PIECE, HD), BF16),
        in_specs=[
            pl.BlockSpec(memory_space=pltpu.SMEM),
            pl.BlockSpec(memory_space=pltpu.VMEM),
            pl.BlockSpec(memory_space=pltpu.VMEM),
        ],
        out_specs=pl.BlockSpec(memory_space=pltpu.VMEM),
        compiler_params=pltpu.CompilerParams(vmem_limit_bytes=8 * MIB),
        name="pack",
    )(count, keys, values)


def stack_kernel(in_ref, out_ref):
    held = jnp.full((PIECE, HD), MARK, F32)
    for t in range(SHARDS):
        out_ref[t] = held.astype(BF16)
        x = in_ref[t].astype(F32)
        held = jnp.where(x < MARK_MIN, x, held)


def stack(pieces):
    return pl.pallas_call(
        stack_kernel,
        out_shape=jax.ShapeDtypeStruct((SHARDS, PIECE, HD), BF16),
        in_specs=[pl.BlockSpec(memory_space=pltpu.VMEM)],
        out_specs=pl.BlockSpec(memory_space=pltpu.VMEM),
        compiler_params=pltpu.CompilerParams(vmem_limit_bytes=8 * MIB),
        name="stack",
    )(pieces)


def segsum_kernel(flag_ref, in_ref, out_ref):
    total = jnp.zeros((PIECE, HD), F32)
    for t in range(SHARDS - 1, -1, -1):
        here = flag_ref[t].astype(F32) < MARK_MIN
        out_ref[t] = jnp.where(here, total, 0.0).astype(BF16)
        total = jnp.where(here, 0.0, total) + in_ref[t].astype(F32)


def segsum(flags, pieces):
    return pl.pallas_call(
        segsum_kernel,
        out_shape=jax.ShapeDtypeStruct((SHARDS, PIECE, HD), BF16),
        in_specs=[pl.BlockSpec(memory_space=pltpu.VMEM)] * 2,
        out_specs=pl.BlockSpec(memory_space=pltpu.VMEM),
        compiler_params=pltpu.CompilerParams(vmem_limit_bytes=8 * MIB),
        name="segsum",
    )(flags, pieces)


def final_kernel(count_ref, dk_ref, dv_ref, in_ref, gk_ref, gv_ref, acc):
    for half, (ref, out, scale) in enumerate(((dk_ref, gk_ref, SCALE), (dv_ref, gv_ref, 1.0))):
        acc[...] = ref[...]
        piece = in_ref[pl.ds(half * 16, 16)].astype(F32)
        for j in range(MAXA):
            last = last_of_depth(count_ref, j)
            row = pl.multiple_of(jnp.maximum(last, 0) * BLK, BLK)
            term = piece[:, 8 * j : 8 * j + 8, :].reshape(BLK, HD)
            acc[pl.ds(row, BLK), :] += jnp.where(last >= 0, term, 0.0)
        out[...] = (acc[...] * scale).astype(BF16)


def final(count, dk, dv, pieces):
    shape = jax.ShapeDtypeStruct((OWN * BLK, HD), BF16)
    return pl.pallas_call(
        final_kernel,
        out_shape=(shape, shape),
        in_specs=[pl.BlockSpec(memory_space=pltpu.SMEM)] + [pl.BlockSpec(memory_space=pltpu.VMEM)] * 3,
        out_specs=[pl.BlockSpec(memory_space=pltpu.VMEM)] * 2,
        scratch_shapes=[pltpu.VMEM((OWN * BLK, HD), F32)],
        compiler_params=pltpu.CompilerParams(vmem_limit_bytes=8 * MIB),
        name="final",
    )(count, dk, dv, pieces)


def nt(a, b):
    return lax.dot_general(a, b, (((1,), (1,)), ((), ())), preferred_element_type=F32)


def nn(a, b):
    return lax.dot_general(a, b, (((1,), (0,)), ((), ())), preferred_element_type=F32)


def tn(a, b):
    return lax.dot_general(a, b, (((0,), (0,)), ((), ())), preferred_element_type=F32)


def attn_kernel(
    ids_ref,
    count_ref,
    base_ref,
    q_ref,
    o_ref,
    k_ref,
    v_ref,
    ext_ref,
    dq_ref,
    dk_ref,
    dv_ref,
    back_ref,
    kt,
    vt,
    dke,
    dve,
    kb,
    vb,
    dka,
    dva,
    *slots,
):
    b = pl.program_id(0)
    base = base_ref[0]

    @pl.when(b == 0)
    def _():
        kt[pl.ds(0, OWN * BLK), :] = k_ref[...]
        vt[pl.ds(0, OWN * BLK), :] = v_ref[...]
        for half, tab in enumerate((kt, vt)):
            piece = ext_ref[pl.ds(half * 16, 16)].astype(F32)
            for j in range(MAXA):
                rows = piece[:, 8 * j : 8 * j + 8, :].reshape(BLK, HD)
                tab[pl.ds((OWN + j) * BLK, BLK), :] = rows.astype(BF16)
        dke[...] = jnp.zeros_like(dke)
        dve[...] = jnp.zeros_like(dve)

    count = count_ref[b]
    coef = SCALE * LOG2E
    heads = CHUNK // HD
    key_pos = lax.broadcasted_iota(jnp.int32, (BLK, CHUNK), 0)
    row_pos = lax.rem(lax.broadcasted_iota(jnp.int32, (BLK, CHUNK), 1), BLK)
    causal = key_pos <= row_pos

    def table_row(j):
        ident = ids_ref[b * MAXA + j]
        place = jnp.where(ident >= base, ident - base, OWN + j)
        return pl.multiple_of(place * BLK, BLK)

    def rows_of(ref, c):
        return jnp.concatenate(
            [ref[:, c * CHUNK + h * HD : c * CHUNK + (h + 1) * HD] for h in range(heads)], axis=0
        )

    def first(n, c):
        e_scr, d_scr, g_scr = slots[3 * (c % 2) : 3 * (c % 2) + 3]
        nk = (n + 1) * BLK
        s_all = nt(kb[pl.ds(0, nk), :], rows_of(q_ref, c))
        d_all = nt(vb[pl.ds(0, nk), :], rows_of(o_ref, c))
        tops, sums, dots = [], [], []
        for j in range(n + 1):
            s = s_all[j * BLK : (j + 1) * BLK]
            d = d_all[j * BLK : (j + 1) * BLK]
            if j == n:
                s = jnp.where(causal, s, -jnp.inf)
            top = jnp.max(s, axis=0, keepdims=True)
            e = jnp.exp2((s - top) * coef)
            tops.append(top)
            sums.append(jnp.sum(e, axis=0, keepdims=True))
            dots.append(jnp.sum(e * d, axis=0, keepdims=True))
            e_scr[pl.ds(j * BLK, BLK), :] = e
            d_scr[pl.ds(j * BLK, BLK), :] = d
        top = functools.reduce(jnp.maximum, tops)
        factors = [jnp.exp2((t - top) * coef) for t in tops]
        inv = 1.0 / sum(f * x for f, x in zip(factors, sums))
        delta = sum(f * x for f, x in zip(factors, dots)) * inv
        for j in range(n + 1):
            g_scr[j : j + 1, :] = factors[j] * inv
        g_scr[MAXA + 1 : MAXA + 2, :] = delta

    def second(n, c):
        e_scr, d_scr, g_scr = slots[3 * (c % 2) : 3 * (c % 2) + 3]
        nk = (n + 1) * BLK
        delta = g_scr[MAXA + 1 : MAXA + 2, :]
        ps, dss = [], []
        for j in range(n + 1):
            p = e_scr[pl.ds(j * BLK, BLK), :] * g_scr[j : j + 1, :]
            ds = p * (d_scr[pl.ds(j * BLK, BLK), :] - delta)
            ps.append(p.astype(BF16))
            dss.append(ds.astype(BF16))
        p_all = jnp.concatenate(ps, axis=0)
        ds_all = jnp.concatenate(dss, axis=0)
        dv = nn(p_all, rows_of(o_ref, c))
        dk = nn(ds_all, rows_of(q_ref, c))
        if c == 0:
            dva[pl.ds(0, nk), :] = dv
            dka[pl.ds(0, nk), :] = dk
        else:
            dva[pl.ds(0, nk), :] += dv
            dka[pl.ds(0, nk), :] += dk
        g = tn(kb[pl.ds(0, nk), :], ds_all) * SCALE
        for h in range(heads):
            at = c * CHUNK + h * HD
            dq_ref[:, at : at + HD] = g[:, h * HD : (h + 1) * HD].T.astype(BF16)

    for n in range(MAXA + 1):

        @pl.when(count == n)
        def _(n=n):
            places = [table_row(j) for j in range(n)] + [pl.multiple_of(b * BLK, BLK)]
            for j in range(n + 1):
                kb[pl.ds(j * BLK, BLK), :] = kt[pl.ds(places[j], BLK), :]
                vb[pl.ds(j * BLK, BLK), :] = vt[pl.ds(places[j], BLK), :]
            chunks = ROWS // CHUNK
            first(n, 0)
            for c in range(chunks):
                if c + 1 < chunks:
                    first(n, c + 1)
                second(n, c)
            for j in range(n + 1):
                dke[pl.ds(places[j], BLK), :] += dka[pl.ds(j * BLK, BLK), :]
                dve[pl.ds(places[j], BLK), :] += dva[pl.ds(j * BLK, BLK), :]

    @pl.when(b == OWN - 1)
    def _():
        dk_ref[...] = dke[pl.ds(0, OWN * BLK), :]
        dv_ref[...] = dve[pl.ds(0, OWN * BLK), :]
        for half, acc in enumerate((dke, dve)):
            parts = [acc[pl.ds((OWN + j) * BLK, BLK), :].reshape(16, 8, HD) for j in range(MAXA)]
            back_ref[pl.ds(half * 16, 16)] = jnp.concatenate(parts, axis=1).astype(BF16)


def attention(ids, count, base, queries, grad_out, keys, values, ext):
    whole = lambda shape: pl.BlockSpec(shape, lambda b, *_: (0,) * len(shape))
    tiles = OWN + MAXA
    return pl.pallas_call(
        attn_kernel,
        grid_spec=pltpu.PrefetchScalarGridSpec(
            num_scalar_prefetch=3,
            grid=(OWN,),
            in_specs=[
                pl.BlockSpec((BLK, ROWS), lambda b, *_: (b, 0)),
                pl.BlockSpec((BLK, ROWS), lambda b, *_: (b, 0)),
                whole((OWN * BLK, HD)),
                whole((OWN * BLK, HD)),
                whole((SHARDS, PIECE, HD)),
            ],
            out_specs=[
                pl.BlockSpec((BLK, ROWS), lambda b, *_: (b, 0)),
                whole((OWN * BLK, HD)),
                whole((OWN * BLK, HD)),
                whole((SHARDS, PIECE, HD)),
            ],
            scratch_shapes=[
                pltpu.VMEM((tiles * BLK, HD), BF16),
                pltpu.VMEM((tiles * BLK, HD), BF16),
                pltpu.VMEM((tiles * BLK, HD), F32),
                pltpu.VMEM((tiles * BLK, HD), F32),
                pltpu.VMEM(((MAXA + 1) * BLK, HD), BF16),
                pltpu.VMEM(((MAXA + 1) * BLK, HD), BF16),
                pltpu.VMEM(((MAXA + 1) * BLK, HD), F32),
                pltpu.VMEM(((MAXA + 1) * BLK, HD), F32),
            ]
            + [
                pltpu.VMEM(((MAXA + 1) * BLK, CHUNK), F32),
                pltpu.VMEM(((MAXA + 1) * BLK, CHUNK), F32),
                pltpu.VMEM((8, CHUNK), F32),
            ]
            * 2,
        ),
        out_shape=(
            jax.ShapeDtypeStruct((OWN * BLK, ROWS), BF16),
            jax.ShapeDtypeStruct((OWN * BLK, HD), F32),
            jax.ShapeDtypeStruct((OWN * BLK, HD), F32),
            jax.ShapeDtypeStruct((SHARDS, PIECE, HD), BF16),
        ),
        compiler_params=pltpu.CompilerParams(vmem_limit_bytes=48 * MIB),
        name="attention",
    )(ids, count, base, queries, grad_out, keys, values, ext)


def body(queries, keys, values, grad_out, ancestor_ids, ancestor_count):
    base = (lax.axis_index("ctx") * OWN).astype(jnp.int32).reshape(1)
    mine = pack(keys, values, ancestor_count)
    pieces = lax.all_to_all(mine, "ctx", 0, 0, tiled=True)
    ext = lax.all_to_all(stack(pieces), "ctx", 0, 0, tiled=True)
    grad_queries, dk, dv, back = attention(
        ancestor_ids.reshape(-1), ancestor_count, base, queries, grad_out, keys, values, ext
    )
    sums = segsum(pieces, lax.all_to_all(back, "ctx", 0, 0, tiled=True))
    terms = lax.all_to_all(sums, "ctx", 0, 0, tiled=True)
    grad_keys, grad_values = final(ancestor_count, dk, dv, terms)
    return (grad_queries, grad_keys, grad_values)


def solution(mesh):
    rows = P(("rep", "ctx"), "head")
    in_specs = (rows, rows, rows, rows, P(("rep", "ctx"), None), P(("rep", "ctx")))
    return jax.shard_map(
        body, mesh=mesh, in_specs=in_specs, out_specs=(rows, rows, rows), check_vma=False
    )
```

```python
import functools

import jax
import jax.numpy as jnp
from jax import lax
from jax.experimental import pallas as pl
from jax.experimental.pallas import tpu as pltpu
from jax.sharding import PartitionSpec as P

HD = 128
HQ = 8
BLK = 128
MAXA = 6
OWN = 8
SHARDS = 32
ROWS = HQ * BLK
CHUNK = 256
PIECE = 8 * MAXA
MARK = 1e30
MARK_MIN = 1e29
SCALE = HD ** (-0.5)
LOG2E = 1.4426950408889634
COEF = SCALE * LOG2E
SPLIT = 5
MIB = 1024 * 1024
VMEM = 56 * MIB
VMEM_EXTERNAL = 50 * MIB
VMEM_STATS = 56 * MIB

F32 = jnp.float32
BF16 = jnp.bfloat16


def last_of_depth(count_ref, depth):
    found = jnp.int32(-1)
    for b in range(OWN):
        found = jnp.where(count_ref[b] == depth, jnp.int32(b), found)
    return found


def pack_kernel(count_ref, k_ref, v_ref, out_ref):
    for half, ref in enumerate((k_ref, v_ref)):
        parts = []
        for j in range(MAXA):
            last = last_of_depth(count_ref, j)
            row = pl.multiple_of(jnp.maximum(last, 0) * BLK, BLK)
            block = ref[pl.ds(row, BLK), :].astype(F32)
            block = jnp.where(last >= 0, block, MARK)
            parts.append(block.reshape(16, 8, HD))
        out_ref[pl.ds(half * 16, 16)] = jnp.concatenate(parts, axis=1).astype(BF16)


def pack(keys, values, count):
    return pl.pallas_call(
        pack_kernel,
        out_shape=jax.ShapeDtypeStruct((SHARDS, PIECE, HD), BF16),
        in_specs=[
            pl.BlockSpec(memory_space=pltpu.SMEM),
            pl.BlockSpec(memory_space=pltpu.VMEM),
            pl.BlockSpec(memory_space=pltpu.VMEM),
        ],
        out_specs=pl.BlockSpec(memory_space=pltpu.VMEM),
        name="pack",
    )(count, keys, values)


def stack_kernel(in_ref, out_ref):
    held = jnp.full((PIECE, HD), MARK, F32)
    for t in range(SHARDS):
        out_ref[t] = held.astype(BF16)
        x = in_ref[t].astype(F32)
        held = jnp.where(x < MARK_MIN, x, held)


def stack(pieces):
    return pl.pallas_call(
        stack_kernel,
        out_shape=jax.ShapeDtypeStruct((SHARDS, PIECE, HD), BF16),
        in_specs=[pl.BlockSpec(memory_space=pltpu.VMEM)],
        out_specs=pl.BlockSpec(memory_space=pltpu.VMEM),
        compiler_params=pltpu.CompilerParams(vmem_limit_bytes=8 * MIB),
        name="stack",
    )(pieces)


def segsum_kernel(flag_ref, in_ref, out_ref):
    total = jnp.zeros((PIECE, HD), F32)
    for t in range(SHARDS - 1, -1, -1):
        here = flag_ref[t].astype(F32) < MARK_MIN
        out_ref[t] = jnp.where(here, total, 0.0).astype(BF16)
        total = jnp.where(here, 0.0, total) + in_ref[t].astype(F32)


def segsum(flags, pieces):
    return pl.pallas_call(
        segsum_kernel,
        out_shape=jax.ShapeDtypeStruct((SHARDS, PIECE, HD), BF16),
        in_specs=[pl.BlockSpec(memory_space=pltpu.VMEM)] * 2,
        out_specs=pl.BlockSpec(memory_space=pltpu.VMEM),
        compiler_params=pltpu.CompilerParams(vmem_limit_bytes=8 * MIB),
        name="segsum",
    )(flags, pieces)


def final_kernel(count_ref, dk_ref, dv_ref, in_ref, gk_ref, gv_ref, acc):
    for half, (ref, out, scale) in enumerate(((dk_ref, gk_ref, SCALE), (dv_ref, gv_ref, 1.0))):
        acc[...] = ref[...]
        piece = in_ref[pl.ds(half * 16, 16)].astype(F32)
        for j in range(MAXA):
            last = last_of_depth(count_ref, j)
            row = pl.multiple_of(jnp.maximum(last, 0) * BLK, BLK)
            term = piece[:, 8 * j : 8 * j + 8, :].reshape(BLK, HD)
            acc[pl.ds(row, BLK), :] += jnp.where(last >= 0, term, 0.0)
        out[...] = (acc[...] * scale).astype(BF16)


def final(count, dk, dv, pieces):
    shape = jax.ShapeDtypeStruct((OWN * BLK, HD), BF16)
    return pl.pallas_call(
        final_kernel,
        out_shape=(shape, shape),
        in_specs=[pl.BlockSpec(memory_space=pltpu.SMEM)] + [pl.BlockSpec(memory_space=pltpu.VMEM)] * 3,
        out_specs=[pl.BlockSpec(memory_space=pltpu.VMEM)] * 2,
        scratch_shapes=[pltpu.VMEM((OWN * BLK, HD), F32)],
        compiler_params=pltpu.CompilerParams(vmem_limit_bytes=8 * MIB),
        name="final",
    )(count, dk, dv, pieces)


def nt(a, b):
    return lax.dot_general(a, b, (((1,), (1,)), ((), ())), preferred_element_type=F32)


def nn(a, b):
    return lax.dot_general(a, b, (((1,), (0,)), ((), ())), preferred_element_type=F32)


def tn(a, b):
    return lax.dot_general(a, b, (((0,), (0,)), ((), ())), preferred_element_type=F32)


def rows_of(ref, c):
    heads = CHUNK // HD
    return jnp.concatenate(
        [ref[:, c * CHUNK + h * HD : c * CHUNK + (h + 1) * HD] for h in range(heads)], axis=0
    )


def chunk_cols(c):
    return slice(c * CHUNK, (c + 1) * CHUNK)


def tile_rows(x, j):
    return x[j * BLK : (j + 1) * BLK]


def causal_mask():
    key_pos = lax.broadcasted_iota(jnp.int32, (BLK, CHUNK), 0)
    row_pos = lax.rem(lax.broadcasted_iota(jnp.int32, (BLK, CHUNK), 1), BLK)
    return key_pos <= row_pos


def external_count(ids_ref, count_ref, base, b):
    found = jnp.int32(0)
    for j in range(MAXA):
        outside = jnp.logical_and(j < count_ref[b], ids_ref[b * MAXA + j] < base)
        found = found + jnp.where(outside, 1, 0).astype(jnp.int32)
    return found


def local_places(ids_ref, base, b, ext, n):
    places = []
    for i in range(n - 1):
        ident = ids_ref[b * MAXA + ext + i]
        places.append(pl.multiple_of((ident - base) * BLK, BLK))
    return places + [pl.multiple_of(b * BLK, BLK)]


def tile_stats(s, d):
    top = jnp.max(s, axis=0, keepdims=True)
    e = jnp.exp2((s - top) * COEF)
    return e, (top, jnp.sum(e, axis=0, keepdims=True), jnp.sum(e * d, axis=0, keepdims=True))


def merge_stats(parts):
    top = functools.reduce(jnp.maximum, [p[0] for p in parts])
    factors = [jnp.exp2((p[0] - top) * COEF) for p in parts]
    total = sum(f * p[1] for f, p in zip(factors, parts))
    dot = sum(f * p[2] for f, p in zip(factors, parts))
    return top, factors, total, dot


def local_kernel(ids_ref, count_ref, base_ref, q_ref, o_ref, k_ref, v_ref, st_ref, kb, vb):
    b = pl.program_id(0)
    base = base_ref[0]
    ext = external_count(ids_ref, count_ref, base, b)
    own = count_ref[b] - ext + 1
    causal = causal_mask()
    for n in range(1, MAXA + 2):

        @pl.when(own == n)
        def _(n=n):
            for j, place in enumerate(local_places(ids_ref, base, b, ext, n)):
                kb[pl.ds(j * BLK, BLK), :] = k_ref[pl.ds(place, BLK), :]
                vb[pl.ds(j * BLK, BLK), :] = v_ref[pl.ds(place, BLK), :]
            nk = n * BLK
            for c in range(ROWS // CHUNK):
                s_all = nt(kb[pl.ds(0, nk), :], rows_of(q_ref, c))
                d_all = nt(vb[pl.ds(0, nk), :], rows_of(o_ref, c))
                parts = []
                for j in range(n):
                    s = tile_rows(s_all, j)
                    if j == n - 1:
                        s = jnp.where(causal, s, -jnp.inf)
                    parts.append(tile_stats(s, tile_rows(d_all, j))[1])
                top, _, total, dot = merge_stats(parts)
                st_ref[0, 0:1, chunk_cols(c)] = top
                st_ref[0, 1:2, chunk_cols(c)] = total
                st_ref[0, 2:3, chunk_cols(c)] = dot


def whole(shape):
    return pl.BlockSpec(shape, lambda b, *_: (0,) * len(shape))


def row_block(first=0):
    return pl.BlockSpec((BLK, ROWS), lambda b, *_: (b + first, 0))


def plane(rows, first=0):
    return pl.BlockSpec((1, rows, ROWS), lambda b, *_: (b + first, 0, 0))


STATS = jax.ShapeDtypeStruct((OWN, 8, ROWS), F32)
TILES = (MAXA + 1) * BLK


def cost(us):
    return pl.CostEstimate(flops=int(us * 1e9), bytes_accessed=6 * MIB, transcendentals=0)


def local_stats(scalars, queries, grad_out, keys, values):
    return pl.pallas_call(
        local_kernel,
        grid_spec=pltpu.PrefetchScalarGridSpec(
            num_scalar_prefetch=3,
            grid=(OWN,),
            in_specs=[row_block(), row_block(), whole((OWN * BLK, HD)), whole((OWN * BLK, HD))],
            out_specs=plane(8),
            scratch_shapes=[pltpu.VMEM((TILES, HD), BF16)] * 2,
        ),
        out_shape=STATS,
        compiler_params=pltpu.CompilerParams(vmem_limit_bytes=VMEM_STATS),
        cost_estimate=cost(10),
        name="local_stats",
    )(*scalars, queries, grad_out, keys, values)


def external_kernel(
    ids_ref,
    count_ref,
    base_ref,
    q_ref,
    o_ref,
    st_ref,
    ext_ref,
    so_ref,
    dqx_ref,
    back_ref,
    kx,
    vx,
    kxt,
    dkx,
    dvx,
    *slots,
):
    b = pl.program_id(0)
    base = base_ref[0]

    @pl.when(b == 0)
    def _():
        for half, tab in enumerate((kx, vx)):
            piece = ext_ref[pl.ds(half * 16, 16)].astype(F32)
            for j in range(MAXA):
                rows = piece[:, 8 * j : 8 * j + 8, :].reshape(BLK, HD)
                tab[pl.ds(j * BLK, BLK), :] = rows.astype(BF16)
                if half == 0:
                    kxt[:, j * BLK : (j + 1) * BLK] = rows.T.astype(BF16)
        dkx[...] = jnp.zeros_like(dkx)
        dvx[...] = jnp.zeros_like(dvx)

    def first(n, c):
        e_scr, d_scr, g_scr = slots[3 * (c % 2) : 3 * (c % 2) + 3]
        cols = chunk_cols(c)
        parts = []
        if n:
            s_all = nt(kx[pl.ds(0, n * BLK), :], rows_of(q_ref, c))
            d_all = nt(vx[pl.ds(0, n * BLK), :], rows_of(o_ref, c))
            for j in range(n):
                d = tile_rows(d_all, j)
                e, stats = tile_stats(tile_rows(s_all, j), d)
                parts.append(stats)
                e_scr[pl.ds(j * BLK, BLK), :] = e
                d_scr[pl.ds(j * BLK, BLK), :] = d
        parts.append(tuple(st_ref[0, i : i + 1, cols] for i in range(3)))
        top, factors, total, dot = merge_stats(parts)
        inv = 1.0 / total
        delta = dot * inv
        for j in range(n):
            g_scr[j : j + 1, :] = factors[j] * inv
        g_scr[MAXA + 1 : MAXA + 2, :] = delta
        so_ref[0, 0:1, cols] = top
        so_ref[0, 1:2, cols] = inv
        so_ref[0, 2:3, cols] = delta

    def second(n, c):
        e_scr, d_scr, g_scr = slots[3 * (c % 2) : 3 * (c % 2) + 3]
        nk = n * BLK
        delta = g_scr[MAXA + 1 : MAXA + 2, :]
        ps, dss = [], []
        for j in range(n):
            p = e_scr[pl.ds(j * BLK, BLK), :] * g_scr[j : j + 1, :]
            ds = p * (d_scr[pl.ds(j * BLK, BLK), :] - delta)
            ps.append(p.astype(BF16))
            dss.append(ds.astype(BF16))
        ds_all = jnp.concatenate(dss, axis=0)
        dvx[pl.ds(0, nk), :] += nn(jnp.concatenate(ps, axis=0), rows_of(o_ref, c))
        dkx[pl.ds(0, nk), :] += nn(ds_all, rows_of(q_ref, c))
        dqx_ref[0, :, chunk_cols(c)] = nn(kxt[:, :nk], ds_all)

    count = external_count(ids_ref, count_ref, base, b)
    chunks = ROWS // CHUNK
    for n in range(MAXA + 1):

        @pl.when(count == n)
        def _(n=n):
            if n == 0:
                for c in range(chunks):
                    first(0, c)
                dqx_ref[...] = jnp.zeros_like(dqx_ref)
                return
            first(n, 0)
            for c in range(chunks):
                if c + 1 < chunks:
                    first(n, c + 1)
                second(n, c)

    @pl.when(b == OWN - 1)
    def _():
        for half, acc in enumerate((dkx, dvx)):
            parts = [acc[pl.ds(j * BLK, BLK), :].reshape(16, 8, HD) for j in range(MAXA)]
            back_ref[pl.ds(half * 16, 16)] = jnp.concatenate(parts, axis=1).astype(BF16)


def external(scalars, queries, grad_out, stats, ext):
    wide = MAXA * BLK
    return pl.pallas_call(
        external_kernel,
        grid_spec=pltpu.PrefetchScalarGridSpec(
            num_scalar_prefetch=3,
            grid=(OWN,),
            in_specs=[row_block(), row_block(), plane(8), whole((SHARDS, PIECE, HD))],
            out_specs=[plane(8), plane(HD), whole((SHARDS, PIECE, HD))],
            scratch_shapes=[
                pltpu.VMEM((wide, HD), BF16),
                pltpu.VMEM((wide, HD), BF16),
                pltpu.VMEM((HD, wide), BF16),
                pltpu.VMEM((wide, HD), F32),
                pltpu.VMEM((wide, HD), F32),
            ]
            + [
                pltpu.VMEM((wide, CHUNK), F32),
                pltpu.VMEM((wide, CHUNK), F32),
                pltpu.VMEM((8, CHUNK), F32),
            ]
            * 2,
        ),
        out_shape=(
            STATS,
            jax.ShapeDtypeStruct((OWN, HD, ROWS), F32),
            jax.ShapeDtypeStruct((SHARDS, PIECE, HD), BF16),
        ),
        compiler_params=pltpu.CompilerParams(vmem_limit_bytes=VMEM_EXTERNAL),
        cost_estimate=cost(16),
        name="external",
    )(*scalars, queries, grad_out, stats, ext)


def own_kernel(
    first_block,
    blocks,
    ids_ref,
    count_ref,
    base_ref,
    q_ref,
    o_ref,
    k_ref,
    v_ref,
    st_ref,
    dqx_ref,
    *refs,
):
    if first_block:
        refs = refs[1:]
        dk_in, dv_in = refs[:2]
        refs = refs[2:]
    dq_ref, dk_ref, dv_ref, kb, vb, dka, dva = refs[:7]
    slots = refs[7:]
    b = pl.program_id(0) + first_block
    base = base_ref[0]

    @pl.when(b == first_block)
    def _():
        if first_block:
            dk_ref[...] = dk_in[...]
            dv_ref[...] = dv_in[...]
        else:
            dk_ref[...] = jnp.zeros_like(dk_ref)
            dv_ref[...] = jnp.zeros_like(dv_ref)

    ext = external_count(ids_ref, count_ref, base, b)
    own = count_ref[b] - ext + 1
    causal = causal_mask()

    def first(n, c):
        p_scr, s_scr = slots[2 * (c % 2) : 2 * (c % 2) + 2]
        cols = chunk_cols(c)
        top, inv, delta = (st_ref[0, i : i + 1, cols] for i in range(3))
        s_all = nt(kb[pl.ds(0, n * BLK), :], rows_of(q_ref, c))
        d_all = nt(vb[pl.ds(0, n * BLK), :], rows_of(o_ref, c))
        for j in range(n):
            s = tile_rows(s_all, j)
            if j == n - 1:
                s = jnp.where(causal, s, -jnp.inf)
            p = jnp.exp2((s - top) * COEF) * inv
            p_scr[pl.ds(j * BLK, BLK), :] = p.astype(BF16)
            s_scr[pl.ds(j * BLK, BLK), :] = (p * (tile_rows(d_all, j) - delta)).astype(BF16)

    def second(n, c):
        p_scr, s_scr = slots[2 * (c % 2) : 2 * (c % 2) + 2]
        nk = n * BLK
        dv = nn(p_scr[pl.ds(0, nk), :], rows_of(o_ref, c))
        dk = nn(s_scr[pl.ds(0, nk), :], rows_of(q_ref, c))
        if c == 0:
            dva[pl.ds(0, nk), :] = dv
            dka[pl.ds(0, nk), :] = dk
        else:
            dva[pl.ds(0, nk), :] += dv
            dka[pl.ds(0, nk), :] += dk
        g = tn(kb[pl.ds(0, nk), :], s_scr[pl.ds(0, nk), :])
        g = (g + dqx_ref[0, :, chunk_cols(c)]) * SCALE
        for h in range(CHUNK // HD):
            at = c * CHUNK + h * HD
            dq_ref[:, at : at + HD] = g[:, h * HD : (h + 1) * HD].T.astype(BF16)

    chunks = ROWS // CHUNK
    for n in range(1, MAXA + 2):

        @pl.when(own == n)
        def _(n=n):
            places = local_places(ids_ref, base, b, ext, n)
            for j in range(n):
                kb[pl.ds(j * BLK, BLK), :] = k_ref[pl.ds(places[j], BLK), :]
                vb[pl.ds(j * BLK, BLK), :] = v_ref[pl.ds(places[j], BLK), :]
            first(n, 0)
            for c in range(chunks):
                if c + 1 < chunks:
                    first(n, c + 1)
                second(n, c)
            for j in range(n):
                dk_ref[pl.ds(places[j], BLK), :] += dka[pl.ds(j * BLK, BLK), :]
                dv_ref[pl.ds(places[j], BLK), :] += dva[pl.ds(j * BLK, BLK), :]


def own_grads(first_block, blocks, scalars, queries, grad_out, keys, values, stats, dqx, *before):
    side = (OWN * BLK, HD)
    more = [pl.BlockSpec(memory_space=pl.ANY), whole(side), whole(side)] if before else []
    return pl.pallas_call(
        functools.partial(own_kernel, first_block, blocks),
        grid_spec=pltpu.PrefetchScalarGridSpec(
            num_scalar_prefetch=3,
            grid=(blocks,),
            in_specs=[
                row_block(first_block),
                row_block(first_block),
                whole(side),
                whole(side),
                plane(8, first_block),
                plane(HD, first_block),
            ]
            + more,
            out_specs=[row_block(first_block), whole(side), whole(side)],
            scratch_shapes=[
                pltpu.VMEM((TILES, HD), BF16),
                pltpu.VMEM((TILES, HD), BF16),
                pltpu.VMEM((TILES, HD), F32),
                pltpu.VMEM((TILES, HD), F32),
            ]
            + [pltpu.VMEM((TILES, CHUNK), BF16)] * 4,
        ),
        out_shape=(
            jax.ShapeDtypeStruct((OWN * BLK, ROWS), BF16),
            jax.ShapeDtypeStruct(side, F32),
            jax.ShapeDtypeStruct(side, F32),
        ),
        input_output_aliases={9: 0} if before else {},
        compiler_params=pltpu.CompilerParams(vmem_limit_bytes=VMEM),
        cost_estimate=cost(10),
        name=f"own_grads_{first_block}",
    )(*scalars, queries, grad_out, keys, values, stats, dqx, *before)


def body(queries, keys, values, grad_out, ancestor_ids, ancestor_count):
    base = (lax.axis_index("ctx") * OWN).astype(jnp.int32).reshape(1)
    scalars = (ancestor_ids.reshape(-1), ancestor_count, base)
    pieces = lax.all_to_all(pack(keys, values, ancestor_count), "ctx", 0, 0, tiled=True)
    stats = local_stats(scalars, queries, grad_out, keys, values)
    ext = lax.all_to_all(stack(pieces), "ctx", 0, 0, tiled=True)
    stats, dqx, back = external(scalars, queries, grad_out, stats, ext)
    inputs = (scalars, queries, grad_out, keys, values, stats, dqx)
    sums = segsum(pieces, lax.all_to_all(back, "ctx", 0, 0, tiled=True))
    grads = own_grads(0, SPLIT, *inputs)
    sums, grads = lax.optimization_barrier((sums, grads))
    terms = lax.all_to_all(sums, "ctx", 0, 0, tiled=True)
    grad_queries, dk, dv = own_grads(SPLIT, OWN - SPLIT, *inputs, *grads)
    grad_keys, grad_values = final(ancestor_count, dk, dv, terms)
    return (grad_queries, grad_keys, grad_values)


def solution(mesh):
    rows = P(("rep", "ctx"), "head")
    in_specs = (rows, rows, rows, rows, P(("rep", "ctx"), None), P(("rep", "ctx")))
    return jax.shard_map(
        body, mesh=mesh, in_specs=in_specs, out_specs=(rows, rows, rows), check_vma=False
    )
```

```python
import functools

import jax
import jax.numpy as jnp
from jax import lax
from jax.experimental import pallas as pl
from jax.experimental.pallas import tpu as pltpu
from jax.sharding import PartitionSpec as P

HD = 128
HQ = 8
BLK = 128
MAXA = 6
OWN = 8
SHARDS = 32
ROWS = HQ * BLK
CHUNK = 256
PIECE = 8 * MAXA
MARK = 1e30
MARK_MIN = 1e29
SCALE = HD ** (-0.5)
LOG2E = 1.4426950408889634
MIB = 1024 * 1024
VMEM_A = 50 * MIB
VMEM_Q = 40 * MIB

F32 = jnp.float32
BF16 = jnp.bfloat16


def last_of_depth(count_ref, depth):
    found = jnp.int32(-1)
    for b in range(OWN):
        found = jnp.where(count_ref[b] == depth, jnp.int32(b), found)
    return found


def pack_kernel(count_ref, k_ref, v_ref, out_ref):
    for half, ref in enumerate((k_ref, v_ref)):
        parts = []
        for j in range(MAXA):
            last = last_of_depth(count_ref, j)
            row = pl.multiple_of(jnp.maximum(last, 0) * BLK, BLK)
            block = ref[pl.ds(row, BLK), :].astype(F32)
            block = jnp.where(last >= 0, block, MARK)
            parts.append(block.reshape(16, 8, HD))
        out_ref[pl.ds(half * 16, 16)] = jnp.concatenate(parts, axis=1).astype(BF16)


def pack(keys, values, count):
    return pl.pallas_call(
        pack_kernel,
        out_shape=jax.ShapeDtypeStruct((SHARDS, PIECE, HD), BF16),
        in_specs=[
            pl.BlockSpec(memory_space=pltpu.SMEM),
            pl.BlockSpec(memory_space=pltpu.VMEM),
            pl.BlockSpec(memory_space=pltpu.VMEM),
        ],
        out_specs=pl.BlockSpec(memory_space=pltpu.VMEM),
        name="pack",
    )(count, keys, values)


def stack_kernel(in_ref, out_ref):
    held = jnp.full((PIECE, HD), MARK, F32)
    for t in range(SHARDS):
        out_ref[t] = held.astype(BF16)
        x = in_ref[t].astype(F32)
        held = jnp.where(x < MARK_MIN, x, held)


def stack(pieces):
    return pl.pallas_call(
        stack_kernel,
        out_shape=jax.ShapeDtypeStruct((SHARDS, PIECE, HD), BF16),
        in_specs=[pl.BlockSpec(memory_space=pltpu.VMEM)],
        out_specs=pl.BlockSpec(memory_space=pltpu.VMEM),
        compiler_params=pltpu.CompilerParams(vmem_limit_bytes=8 * MIB),
        name="stack",
    )(pieces)


def segsum_kernel(flag_ref, in_ref, out_ref):
    total = jnp.zeros((PIECE, HD), F32)
    for t in range(SHARDS - 1, -1, -1):
        here = flag_ref[t].astype(F32) < MARK_MIN
        out_ref[t] = jnp.where(here, total, 0.0).astype(BF16)
        total = jnp.where(here, 0.0, total) + in_ref[t].astype(F32)


def segsum(flags, pieces):
    return pl.pallas_call(
        segsum_kernel,
        out_shape=jax.ShapeDtypeStruct((SHARDS, PIECE, HD), BF16),
        in_specs=[pl.BlockSpec(memory_space=pltpu.VMEM)] * 2,
        out_specs=pl.BlockSpec(memory_space=pltpu.VMEM),
        compiler_params=pltpu.CompilerParams(vmem_limit_bytes=8 * MIB),
        name="segsum",
    )(flags, pieces)


def final_kernel(count_ref, dk_ref, dv_ref, in_ref, gk_ref, gv_ref, acc):
    for half, (ref, out, scale) in enumerate(((dk_ref, gk_ref, SCALE), (dv_ref, gv_ref, 1.0))):
        acc[...] = ref[...]
        piece = in_ref[pl.ds(half * 16, 16)].astype(F32)
        for j in range(MAXA):
            last = last_of_depth(count_ref, j)
            row = pl.multiple_of(jnp.maximum(last, 0) * BLK, BLK)
            term = piece[:, 8 * j : 8 * j + 8, :].reshape(BLK, HD)
            acc[pl.ds(row, BLK), :] += jnp.where(last >= 0, term, 0.0)
        out[...] = (acc[...] * scale).astype(BF16)


def final(count, dk, dv, pieces):
    shape = jax.ShapeDtypeStruct((OWN * BLK, HD), BF16)
    return pl.pallas_call(
        final_kernel,
        out_shape=(shape, shape),
        in_specs=[pl.BlockSpec(memory_space=pltpu.SMEM)] + [pl.BlockSpec(memory_space=pltpu.VMEM)] * 3,
        out_specs=[pl.BlockSpec(memory_space=pltpu.VMEM)] * 2,
        scratch_shapes=[pltpu.VMEM((OWN * BLK, HD), F32)],
        compiler_params=pltpu.CompilerParams(vmem_limit_bytes=8 * MIB),
        name="final",
    )(count, dk, dv, pieces)


def nt(a, b):
    return lax.dot_general(a, b, (((1,), (1,)), ((), ())), preferred_element_type=F32)


def nn(a, b):
    return lax.dot_general(a, b, (((1,), (0,)), ((), ())), preferred_element_type=F32)


def tn(a, b):
    return lax.dot_general(a, b, (((0,), (0,)), ((), ())), preferred_element_type=F32)


def table_place(ids_ref, base, b, j):
    ident = ids_ref[b, j]
    place = jnp.where(ident >= base, ident - base, OWN + j)
    return pl.multiple_of(place * BLK, BLK)


def attn_kernel(
    ids_ref,
    count_ref,
    base_ref,
    q_ref,
    o_ref,
    k_ref,
    v_ref,
    ext_ref,
    ds_ref,
    kt,
    dk_ref,
    dv_ref,
    back_ref,
    vt,
    dke,
    dve,
    kb,
    vb,
    dka,
    dva,
    *slots,
):
    b = pl.program_id(0)
    base = base_ref[0]

    @pl.when(b == 0)
    def _():
        kt[pl.ds(0, OWN * BLK), :] = k_ref[...]
        vt[pl.ds(0, OWN * BLK), :] = v_ref[...]
        for half, tab in enumerate((kt, vt)):
            piece = ext_ref[pl.ds(half * 16, 16)].astype(F32)
            for j in range(MAXA):
                rows = piece[:, 8 * j : 8 * j + 8, :].reshape(BLK, HD)
                tab[pl.ds((OWN + j) * BLK, BLK), :] = rows.astype(BF16)
        dke[...] = jnp.zeros_like(dke)
        dve[...] = jnp.zeros_like(dve)

    count = count_ref[b]
    coef = SCALE * LOG2E
    heads = CHUNK // HD
    key_pos = lax.broadcasted_iota(jnp.int32, (BLK, CHUNK), 0)
    row_pos = lax.rem(lax.broadcasted_iota(jnp.int32, (BLK, CHUNK), 1), BLK)
    causal = key_pos <= row_pos

    def table_row(j):
        return table_place(ids_ref, base, b, j)

    def rows_of(ref, c):
        return jnp.concatenate(
            [ref[:, c * CHUNK + h * HD : c * CHUNK + (h + 1) * HD] for h in range(heads)], axis=0
        )

    def first(n, c):
        e_scr, d_scr, g_scr = slots[3 * (c % 2) : 3 * (c % 2) + 3]
        nk = (n + 1) * BLK
        s_all = nt(kb[pl.ds(0, nk), :], rows_of(q_ref, c))
        d_all = nt(vb[pl.ds(0, nk), :], rows_of(o_ref, c))
        tops, sums, dots = [], [], []
        for j in range(n + 1):
            s = s_all[j * BLK : (j + 1) * BLK]
            d = d_all[j * BLK : (j + 1) * BLK]
            if j == n:
                s = jnp.where(causal, s, -jnp.inf)
            top = jnp.max(s, axis=0, keepdims=True)
            e = jnp.exp2((s - top) * coef)
            tops.append(top)
            sums.append(jnp.sum(e, axis=0, keepdims=True))
            dots.append(jnp.sum(e * d, axis=0, keepdims=True))
            e_scr[pl.ds(j * BLK, BLK), :] = e
            d_scr[pl.ds(j * BLK, BLK), :] = d
        top = functools.reduce(jnp.maximum, tops)
        factors = [jnp.exp2((t - top) * coef) for t in tops]
        inv = 1.0 / sum(f * x for f, x in zip(factors, sums))
        delta = sum(f * x for f, x in zip(factors, dots)) * inv
        for j in range(n + 1):
            g_scr[j : j + 1, :] = factors[j] * inv
        g_scr[MAXA + 1 : MAXA + 2, :] = delta

    def second(n, c):
        e_scr, d_scr, g_scr = slots[3 * (c % 2) : 3 * (c % 2) + 3]
        nk = (n + 1) * BLK
        delta = g_scr[MAXA + 1 : MAXA + 2, :]
        ps, dss = [], []
        for j in range(n + 1):
            p = e_scr[pl.ds(j * BLK, BLK), :] * g_scr[j : j + 1, :]
            ds = p * (d_scr[pl.ds(j * BLK, BLK), :] - delta)
            ps.append(p.astype(BF16))
            dss.append(ds.astype(BF16))
            ds_ref[0, pl.ds(j * BLK, BLK), c * CHUNK : (c + 1) * CHUNK] = dss[-1]
        p_all = jnp.concatenate(ps, axis=0)
        ds_all = jnp.concatenate(dss, axis=0)
        dv = nn(p_all, rows_of(o_ref, c))
        dk = nn(ds_all, rows_of(q_ref, c))
        if c == 0:
            dva[pl.ds(0, nk), :] = dv
            dka[pl.ds(0, nk), :] = dk
        else:
            dva[pl.ds(0, nk), :] += dv
            dka[pl.ds(0, nk), :] += dk

    for n in range(MAXA + 1):

        @pl.when(count == n)
        def _(n=n):
            places = [table_row(j) for j in range(n)] + [pl.multiple_of(b * BLK, BLK)]
            for j in range(n + 1):
                kb[pl.ds(j * BLK, BLK), :] = kt[pl.ds(places[j], BLK), :]
                vb[pl.ds(j * BLK, BLK), :] = vt[pl.ds(places[j], BLK), :]
            chunks = ROWS // CHUNK
            first(n, 0)
            for c in range(chunks):
                if c + 1 < chunks:
                    first(n, c + 1)
                second(n, c)
            for j in range(n + 1):
                dke[pl.ds(places[j], BLK), :] += dka[pl.ds(j * BLK, BLK), :]
                dve[pl.ds(places[j], BLK), :] += dva[pl.ds(j * BLK, BLK), :]

    @pl.when(b == OWN - 1)
    def _():
        dk_ref[...] = dke[pl.ds(0, OWN * BLK), :]
        dv_ref[...] = dve[pl.ds(0, OWN * BLK), :]
        for half, acc in enumerate((dke, dve)):
            parts = [acc[pl.ds((OWN + j) * BLK, BLK), :].reshape(16, 8, HD) for j in range(MAXA)]
            back_ref[pl.ds(half * 16, 16)] = jnp.concatenate(parts, axis=1).astype(BF16)


def attention(ids, count, base, queries, grad_out, keys, values, ext):
    whole = lambda shape: pl.BlockSpec(shape, lambda b, *_: (0,) * len(shape))
    tiles = OWN + MAXA
    return pl.pallas_call(
        attn_kernel,
        grid_spec=pltpu.PrefetchScalarGridSpec(
            num_scalar_prefetch=3,
            grid=(OWN,),
            in_specs=[
                pl.BlockSpec((BLK, ROWS), lambda b, *_: (b, 0)),
                pl.BlockSpec((BLK, ROWS), lambda b, *_: (b, 0)),
                whole((OWN * BLK, HD)),
                whole((OWN * BLK, HD)),
                whole((SHARDS, PIECE, HD)),
            ],
            out_specs=[
                pl.BlockSpec((1, (MAXA + 1) * BLK, ROWS), lambda b, *_: (b, 0, 0)),
                whole((tiles * BLK, HD)),
                whole((OWN * BLK, HD)),
                whole((OWN * BLK, HD)),
                whole((SHARDS, PIECE, HD)),
            ],
            scratch_shapes=[
                pltpu.VMEM((tiles * BLK, HD), BF16),
                pltpu.VMEM((tiles * BLK, HD), F32),
                pltpu.VMEM((tiles * BLK, HD), F32),
                pltpu.VMEM(((MAXA + 1) * BLK, HD), BF16),
                pltpu.VMEM(((MAXA + 1) * BLK, HD), BF16),
                pltpu.VMEM(((MAXA + 1) * BLK, HD), F32),
                pltpu.VMEM(((MAXA + 1) * BLK, HD), F32),
            ]
            + [
                pltpu.VMEM(((MAXA + 1) * BLK, CHUNK), F32),
                pltpu.VMEM(((MAXA + 1) * BLK, CHUNK), F32),
                pltpu.VMEM((8, CHUNK), F32),
            ]
            * 2,
        ),
        out_shape=(
            jax.ShapeDtypeStruct((OWN, (MAXA + 1) * BLK, ROWS), BF16),
            jax.ShapeDtypeStruct((tiles * BLK, HD), BF16),
            jax.ShapeDtypeStruct((OWN * BLK, HD), F32),
            jax.ShapeDtypeStruct((OWN * BLK, HD), F32),
            jax.ShapeDtypeStruct((SHARDS, PIECE, HD), BF16),
        ),
        compiler_params=pltpu.CompilerParams(vmem_limit_bytes=VMEM_A),
        name="attention",
    )(ids, count, base, queries, grad_out, keys, values, ext)


def query_kernel(ids_ref, count_ref, base_ref, ds_ref, kt_ref, dq_ref, kb):
    b = pl.program_id(0)
    count = count_ref[b]
    for n in range(MAXA + 1):

        @pl.when(count == n)
        def _(n=n):
            places = [table_place(ids_ref, base_ref[0], b, j) for j in range(n)]
            places.append(pl.multiple_of(b * BLK, BLK))
            for j in range(n + 1):
                kb[pl.ds(j * BLK, BLK), :] = kt_ref[pl.ds(places[j], BLK), :]
            nk = (n + 1) * BLK
            g = tn(kb[pl.ds(0, nk), :], ds_ref[0, pl.ds(0, nk), :]) * SCALE
            for h in range(HQ):
                head = slice(h * HD, (h + 1) * HD)
                dq_ref[:, head] = g[:, head].T.astype(BF16)


def query_grads(ids, count, base, dscores, table):
    return pl.pallas_call(
        query_kernel,
        grid_spec=pltpu.PrefetchScalarGridSpec(
            num_scalar_prefetch=3,
            grid=(OWN,),
            in_specs=[
                pl.BlockSpec((1, (MAXA + 1) * BLK, ROWS), lambda b, *_: (b, 0, 0)),
                pl.BlockSpec(table.shape, lambda b, *_: (0, 0)),
            ],
            out_specs=pl.BlockSpec((BLK, ROWS), lambda b, *_: (b, 0)),
            scratch_shapes=[pltpu.VMEM(((MAXA + 1) * BLK, HD), BF16)],
        ),
        out_shape=jax.ShapeDtypeStruct((OWN * BLK, ROWS), BF16),
        compiler_params=pltpu.CompilerParams(vmem_limit_bytes=VMEM_Q),
        cost_estimate=pl.CostEstimate(
            flops=int(1e10), bytes_accessed=16 * MIB, transcendentals=0
        ),
        name="query_grads",
    )(ids, count, base, dscores, table)


def body(queries, keys, values, grad_out, ancestor_ids, ancestor_count):
    base = (lax.axis_index("ctx") * OWN).astype(jnp.int32).reshape(1)
    mine = pack(keys, values, ancestor_count)
    pieces = lax.all_to_all(mine, "ctx", 0, 0, tiled=True)
    ext = lax.all_to_all(stack(pieces), "ctx", 0, 0, tiled=True)
    scalars = (ancestor_ids, ancestor_count, base)
    dscores, table, dk, dv, back = attention(*scalars, queries, grad_out, keys, values, ext)
    grad_queries = query_grads(*scalars, dscores, table)
    sums = segsum(pieces, lax.all_to_all(back, "ctx", 0, 0, tiled=True))
    terms = lax.all_to_all(sums, "ctx", 0, 0, tiled=True)
    grad_keys, grad_values = final(ancestor_count, dk, dv, terms)
    return (grad_queries, grad_keys, grad_values)


def solution(mesh):
    rows = P(("rep", "ctx"), "head")
    in_specs = (rows, rows, rows, rows, P(("rep", "ctx"), None), P(("rep", "ctx")))
    return jax.shard_map(
        body, mesh=mesh, in_specs=in_specs, out_specs=(rows, rows, rows), check_vma=False
    )
```

```python
import functools

import jax
import jax.numpy as jnp
from jax import lax
from jax.experimental import pallas as pl
from jax.experimental.pallas import tpu as pltpu
from jax.sharding import PartitionSpec as P

HD = 128
HQ = 8
BLK = 128
MAXA = 6
OWN = 8
SHARDS = 32
ROWS = HQ * BLK
CHUNK = 512
PIECE = 8 * MAXA
MARK = 1e30
MARK_MIN = 1e29
SCALE = HD ** (-0.5)
LOG2E = 1.4426950408889634
MIB = 1024 * 1024
VMEM_A = 50 * MIB
VMEM_Q = 40 * MIB

F32 = jnp.float32
BF16 = jnp.bfloat16


def last_of_depth(count_ref, depth):
    found = jnp.int32(-1)
    for b in range(OWN):
        found = jnp.where(count_ref[b] == depth, jnp.int32(b), found)
    return found


def pack_kernel(count_ref, k_ref, v_ref, out_ref):
    for half, ref in enumerate((k_ref, v_ref)):
        parts = []
        for j in range(MAXA):
            last = last_of_depth(count_ref, j)
            row = pl.multiple_of(jnp.maximum(last, 0) * BLK, BLK)
            block = ref[pl.ds(row, BLK), :].astype(F32)
            block = jnp.where(last >= 0, block, MARK)
            parts.append(block.reshape(16, 8, HD))
        out_ref[pl.ds(half * 16, 16)] = jnp.concatenate(parts, axis=1).astype(BF16)


def pack(keys, values, count):
    return pl.pallas_call(
        pack_kernel,
        out_shape=jax.ShapeDtypeStruct((SHARDS, PIECE, HD), BF16),
        in_specs=[
            pl.BlockSpec(memory_space=pltpu.SMEM),
            pl.BlockSpec(memory_space=pltpu.VMEM),
            pl.BlockSpec(memory_space=pltpu.VMEM),
        ],
        out_specs=pl.BlockSpec(memory_space=pltpu.VMEM),
        name="pack",
    )(count, keys, values)


def stack_kernel(in_ref, out_ref):
    held = jnp.full((PIECE, HD), MARK, F32)
    for t in range(SHARDS):
        out_ref[t] = held.astype(BF16)
        x = in_ref[t].astype(F32)
        held = jnp.where(x < MARK_MIN, x, held)


def stack(pieces):
    return pl.pallas_call(
        stack_kernel,
        out_shape=jax.ShapeDtypeStruct((SHARDS, PIECE, HD), BF16),
        in_specs=[pl.BlockSpec(memory_space=pltpu.VMEM)],
        out_specs=pl.BlockSpec(memory_space=pltpu.VMEM),
        compiler_params=pltpu.CompilerParams(vmem_limit_bytes=8 * MIB),
        name="stack",
    )(pieces)


def segsum_kernel(flag_ref, in_ref, out_ref):
    total = jnp.zeros((PIECE, HD), F32)
    for t in range(SHARDS - 1, -1, -1):
        here = flag_ref[t].astype(F32) < MARK_MIN
        out_ref[t] = jnp.where(here, total, 0.0).astype(BF16)
        total = jnp.where(here, 0.0, total) + in_ref[t].astype(F32)


def segsum(flags, pieces):
    return pl.pallas_call(
        segsum_kernel,
        out_shape=jax.ShapeDtypeStruct((SHARDS, PIECE, HD), BF16),
        in_specs=[pl.BlockSpec(memory_space=pltpu.VMEM)] * 2,
        out_specs=pl.BlockSpec(memory_space=pltpu.VMEM),
        compiler_params=pltpu.CompilerParams(vmem_limit_bytes=8 * MIB),
        name="segsum",
    )(flags, pieces)


def final_kernel(count_ref, dk_ref, dv_ref, in_ref, gk_ref, gv_ref, acc):
    for half, (ref, out, scale) in enumerate(((dk_ref, gk_ref, SCALE), (dv_ref, gv_ref, 1.0))):
        acc[...] = ref[...]
        piece = in_ref[pl.ds(half * 16, 16)].astype(F32)
        for j in range(MAXA):
            last = last_of_depth(count_ref, j)
            row = pl.multiple_of(jnp.maximum(last, 0) * BLK, BLK)
            term = piece[:, 8 * j : 8 * j + 8, :].reshape(BLK, HD)
            acc[pl.ds(row, BLK), :] += jnp.where(last >= 0, term, 0.0)
        out[...] = (acc[...] * scale).astype(BF16)


def final(count, dk, dv, pieces):
    shape = jax.ShapeDtypeStruct((OWN * BLK, HD), BF16)
    return pl.pallas_call(
        final_kernel,
        out_shape=(shape, shape),
        in_specs=[pl.BlockSpec(memory_space=pltpu.SMEM)] + [pl.BlockSpec(memory_space=pltpu.VMEM)] * 3,
        out_specs=[pl.BlockSpec(memory_space=pltpu.VMEM)] * 2,
        scratch_shapes=[pltpu.VMEM((OWN * BLK, HD), F32)],
        compiler_params=pltpu.CompilerParams(vmem_limit_bytes=8 * MIB),
        name="final",
    )(count, dk, dv, pieces)


def nt(a, b):
    return lax.dot_general(a, b, (((1,), (1,)), ((), ())), preferred_element_type=F32)


def nn(a, b):
    return lax.dot_general(a, b, (((1,), (0,)), ((), ())), preferred_element_type=F32)


def tn(a, b):
    return lax.dot_general(a, b, (((0,), (0,)), ((), ())), preferred_element_type=F32)


def table_place(ids_ref, base, b, j):
    ident = ids_ref[b, j]
    place = jnp.where(ident >= base, ident - base, OWN + j)
    return pl.multiple_of(place * BLK, BLK)


def attn_kernel(
    ids_ref,
    count_ref,
    q_ref,
    o_ref,
    k_ref,
    v_ref,
    ext_ref,
    ds_ref,
    kt,
    dk_ref,
    dv_ref,
    back_ref,
    vt,
    dke,
    dve,
    kb,
    vb,
    dka,
    dva,
    *slots,
):
    b = pl.program_id(0)
    base = lax.axis_index("ctx") * OWN

    @pl.when(b == 0)
    def _():
        kt[pl.ds(0, OWN * BLK), :] = k_ref[...]
        vt[pl.ds(0, OWN * BLK), :] = v_ref[...]
        for half, tab in enumerate((kt, vt)):
            piece = ext_ref[pl.ds(half * 16, 16)].astype(F32)
            for j in range(MAXA):
                rows = piece[:, 8 * j : 8 * j + 8, :].reshape(BLK, HD)
                tab[pl.ds((OWN + j) * BLK, BLK), :] = rows.astype(BF16)
        dke[...] = jnp.zeros_like(dke)
        dve[...] = jnp.zeros_like(dve)

    count = count_ref[b]
    coef = SCALE * LOG2E
    heads = CHUNK // HD
    key_pos = lax.broadcasted_iota(jnp.int32, (BLK, CHUNK), 0)
    row_pos = lax.rem(lax.broadcasted_iota(jnp.int32, (BLK, CHUNK), 1), BLK)
    causal = key_pos <= row_pos

    def table_row(j):
        return table_place(ids_ref, base, b, j)

    def rows_of(ref, c):
        return jnp.concatenate(
            [ref[:, c * CHUNK + h * HD : c * CHUNK + (h + 1) * HD] for h in range(heads)], axis=0
        )

    def slot(c):
        return slots[3 * (c % 2) : 3 * (c % 2) + 3]

    def scores(n, c):
        nk = (n + 1) * BLK
        return nt(kb[pl.ds(0, nk), :], rows_of(q_ref, c)), nt(vb[pl.ds(0, nk), :], rows_of(o_ref, c))

    def keep(n, c, j, both):
        e_scr, d_scr, _ = slot(c)
        s, d = (x[j * BLK : (j + 1) * BLK] for x in both)
        if j == n:
            s = jnp.where(causal, s, -jnp.inf)
        top = jnp.max(s, axis=0, keepdims=True)
        e = jnp.exp2((s - top) * coef)
        e_scr[pl.ds(j * BLK, BLK), :] = e
        d_scr[pl.ds(j * BLK, BLK), :] = d
        return top, jnp.sum(e, axis=0, keepdims=True), jnp.sum(e * d, axis=0, keepdims=True)

    def merge(c, stats):
        g_scr = slot(c)[2]
        top = functools.reduce(jnp.maximum, [t for t, _, _ in stats])
        factors = [jnp.exp2((t - top) * coef) for t, _, _ in stats]
        inv = 1.0 / sum(f * x for f, (_, x, _) in zip(factors, stats))
        delta = sum(f * x for f, (_, _, x) in zip(factors, stats)) * inv
        for j, f in enumerate(factors):
            g_scr[j : j + 1, :] = f * inv
        g_scr[MAXA + 1 : MAXA + 2, :] = delta

    def weigh(c, j):
        e_scr, d_scr, g_scr = slot(c)
        p = e_scr[pl.ds(j * BLK, BLK), :] * g_scr[j : j + 1, :]
        ds = p * (d_scr[pl.ds(j * BLK, BLK), :] - g_scr[MAXA + 1 : MAXA + 2, :])
        ds = ds.astype(BF16)
        ds_ref[0, pl.ds(j * BLK, BLK), c * CHUNK : (c + 1) * CHUNK] = ds
        return p.astype(BF16), ds

    def add(n, c, tiles):
        nk = (n + 1) * BLK
        dv = nn(jnp.concatenate([p for p, _ in tiles], axis=0), rows_of(o_ref, c))
        dk = nn(jnp.concatenate([ds for _, ds in tiles], axis=0), rows_of(q_ref, c))
        if c == 0:
            dva[pl.ds(0, nk), :] = dv
            dka[pl.ds(0, nk), :] = dk
        else:
            dva[pl.ds(0, nk), :] += dv
            dka[pl.ds(0, nk), :] += dk

    for n in range(MAXA + 1):

        @pl.when(count == n)
        def _(n=n):
            places = [table_row(j) for j in range(n)] + [pl.multiple_of(b * BLK, BLK)]
            for j in range(n + 1):
                kb[pl.ds(j * BLK, BLK), :] = kt[pl.ds(places[j], BLK), :]
                vb[pl.ds(j * BLK, BLK), :] = vt[pl.ds(places[j], BLK), :]
            chunks = ROWS // CHUNK
            both = scores(n, 0)
            merge(0, [keep(n, 0, j, both) for j in range(n + 1)])
            for c in range(chunks):
                more = c + 1 < chunks
                if more:
                    both = scores(n, c + 1)
                tiles, stats = [], []
                for j in range(n + 1):
                    tiles.append(weigh(c, j))
                    if more:
                        stats.append(keep(n, c + 1, j, both))
                add(n, c, tiles)
                if more:
                    merge(c + 1, stats)
            for j in range(n + 1):
                dke[pl.ds(places[j], BLK), :] += dka[pl.ds(j * BLK, BLK), :]
                dve[pl.ds(places[j], BLK), :] += dva[pl.ds(j * BLK, BLK), :]

    @pl.when(b == OWN - 1)
    def _():
        dk_ref[...] = dke[pl.ds(0, OWN * BLK), :]
        dv_ref[...] = dve[pl.ds(0, OWN * BLK), :]
        for half, acc in enumerate((dke, dve)):
            parts = [acc[pl.ds((OWN + j) * BLK, BLK), :].reshape(16, 8, HD) for j in range(MAXA)]
            back_ref[pl.ds(half * 16, 16)] = jnp.concatenate(parts, axis=1).astype(BF16)


def attention(ids, count, queries, grad_out, keys, values, ext):
    whole = lambda shape: pl.BlockSpec(shape, lambda b, *_: (0,) * len(shape))
    tiles = OWN + MAXA
    return pl.pallas_call(
        attn_kernel,
        grid_spec=pltpu.PrefetchScalarGridSpec(
            num_scalar_prefetch=2,
            grid=(OWN,),
            in_specs=[
                pl.BlockSpec((BLK, ROWS), lambda b, *_: (b, 0)),
                pl.BlockSpec((BLK, ROWS), lambda b, *_: (b, 0)),
                whole((OWN * BLK, HD)),
                whole((OWN * BLK, HD)),
                whole((SHARDS, PIECE, HD)),
            ],
            out_specs=[
                pl.BlockSpec((1, (MAXA + 1) * BLK, ROWS), lambda b, *_: (b, 0, 0)),
                whole((tiles * BLK, HD)),
                whole((OWN * BLK, HD)),
                whole((OWN * BLK, HD)),
                whole((SHARDS, PIECE, HD)),
            ],
            scratch_shapes=[
                pltpu.VMEM((tiles * BLK, HD), BF16),
                pltpu.VMEM((tiles * BLK, HD), F32),
                pltpu.VMEM((tiles * BLK, HD), F32),
                pltpu.VMEM(((MAXA + 1) * BLK, HD), BF16),
                pltpu.VMEM(((MAXA + 1) * BLK, HD), BF16),
                pltpu.VMEM(((MAXA + 1) * BLK, HD), F32),
                pltpu.VMEM(((MAXA + 1) * BLK, HD), F32),
            ]
            + [
                pltpu.VMEM(((MAXA + 1) * BLK, CHUNK), F32),
                pltpu.VMEM(((MAXA + 1) * BLK, CHUNK), F32),
                pltpu.VMEM((8, CHUNK), F32),
            ]
            * 2,
        ),
        out_shape=(
            jax.ShapeDtypeStruct((OWN, (MAXA + 1) * BLK, ROWS), BF16),
            jax.ShapeDtypeStruct((tiles * BLK, HD), BF16),
            jax.ShapeDtypeStruct((OWN * BLK, HD), F32),
            jax.ShapeDtypeStruct((OWN * BLK, HD), F32),
            jax.ShapeDtypeStruct((SHARDS, PIECE, HD), BF16),
        ),
        compiler_params=pltpu.CompilerParams(vmem_limit_bytes=VMEM_A),
        name="attention",
    )(ids, count, queries, grad_out, keys, values, ext)


def query_kernel(ids_ref, count_ref, ds_ref, kt_ref, dq_ref, kb):
    b = pl.program_id(0)
    base = lax.axis_index("ctx") * OWN
    count = count_ref[b]
    for n in range(MAXA + 1):

        @pl.when(count == n)
        def _(n=n):
            places = [table_place(ids_ref, base, b, j) for j in range(n)]
            places.append(pl.multiple_of(b * BLK, BLK))
            for j in range(n + 1):
                kb[pl.ds(j * BLK, BLK), :] = kt_ref[pl.ds(places[j], BLK), :]
            nk = (n + 1) * BLK
            g = tn(kb[pl.ds(0, nk), :], ds_ref[0, pl.ds(0, nk), :]) * SCALE
            for h in range(HQ):
                head = slice(h * HD, (h + 1) * HD)
                dq_ref[:, head] = g[:, head].T.astype(BF16)


def query_grads(ids, count, dscores, table):
    return pl.pallas_call(
        query_kernel,
        grid_spec=pltpu.PrefetchScalarGridSpec(
            num_scalar_prefetch=2,
            grid=(OWN,),
            in_specs=[
                pl.BlockSpec((1, (MAXA + 1) * BLK, ROWS), lambda b, *_: (b, 0, 0)),
                pl.BlockSpec(table.shape, lambda b, *_: (0, 0)),
            ],
            out_specs=pl.BlockSpec((BLK, ROWS), lambda b, *_: (b, 0)),
            scratch_shapes=[pltpu.VMEM(((MAXA + 1) * BLK, HD), BF16)],
        ),
        out_shape=jax.ShapeDtypeStruct((OWN * BLK, ROWS), BF16),
        compiler_params=pltpu.CompilerParams(vmem_limit_bytes=VMEM_Q),
        cost_estimate=pl.CostEstimate(
            flops=int(1e10), bytes_accessed=16 * MIB, transcendentals=0
        ),
        name="query_grads",
    )(ids, count, dscores, table)


def body(queries, keys, values, grad_out, ancestor_ids, ancestor_count):
    mine = pack(keys, values, ancestor_count)
    pieces = lax.all_to_all(mine, "ctx", 0, 0, tiled=True)
    ext = lax.all_to_all(stack(pieces), "ctx", 0, 0, tiled=True)
    scalars = (ancestor_ids, ancestor_count)
    dscores, table, dk, dv, back = attention(*scalars, queries, grad_out, keys, values, ext)
    grad_queries = query_grads(*scalars, dscores, table)
    sums = segsum(pieces, lax.all_to_all(back, "ctx", 0, 0, tiled=True))
    terms = lax.all_to_all(sums, "ctx", 0, 0, tiled=True)
    grad_keys, grad_values = final(ancestor_count, dk, dv, terms)
    return (grad_queries, grad_keys, grad_values)


def solution(mesh):
    rows = P(("rep", "ctx"), "head")
    in_specs = (rows, rows, rows, rows, P(("rep", "ctx"), None), P(("rep", "ctx")))
    return jax.shard_map(
        body, mesh=mesh, in_specs=in_specs, out_specs=(rows, rows, rows), check_vma=False
    )
```

```python
import functools

import jax
import jax.numpy as jnp
from jax import lax
from jax.experimental import pallas as pl
from jax.experimental.pallas import tpu as pltpu
from jax.sharding import PartitionSpec as P

HD = 128
HQ = 8
BLK = 128
MAXA = 6
OWN = 8
SHARDS = 32
ROWS = HQ * BLK
CHUNK = 512
PIECE = 8 * MAXA
MARK = 1e30
MARK_MIN = 1e29
SCALE = HD ** (-0.5)
LOG2E = 1.4426950408889634
MIB = 1024 * 1024
VMEM_A = 50 * MIB
VMEM_Q = 40 * MIB

F32 = jnp.float32
BF16 = jnp.bfloat16


def last_of_depth(count_ref, depth):
    found = jnp.int32(-1)
    for b in range(OWN):
        found = jnp.where(count_ref[b] == depth, jnp.int32(b), found)
    return found


def pack_kernel(count_ref, k_ref, v_ref, out_ref):
    for half, ref in enumerate((k_ref, v_ref)):
        parts = []
        for j in range(MAXA):
            last = last_of_depth(count_ref, j)
            row = pl.multiple_of(jnp.maximum(last, 0) * BLK, BLK)
            block = ref[pl.ds(row, BLK), :].astype(F32)
            block = jnp.where(last >= 0, block, MARK)
            parts.append(block.reshape(16, 8, HD))
        out_ref[pl.ds(half * 16, 16)] = jnp.concatenate(parts, axis=1).astype(BF16)


def pack(keys, values, count):
    return pl.pallas_call(
        pack_kernel,
        out_shape=jax.ShapeDtypeStruct((SHARDS, PIECE, HD), BF16),
        in_specs=[
            pl.BlockSpec(memory_space=pltpu.SMEM),
            pl.BlockSpec(memory_space=pltpu.VMEM),
            pl.BlockSpec(memory_space=pltpu.VMEM),
        ],
        out_specs=pl.BlockSpec(memory_space=pltpu.VMEM),
        name="pack",
    )(count, keys, values)


def stack_kernel(in_ref, out_ref):
    held = jnp.full((PIECE, HD), MARK, F32)
    for t in range(SHARDS):
        out_ref[t] = held.astype(BF16)
        x = in_ref[t].astype(F32)
        held = jnp.where(x < MARK_MIN, x, held)


def stack(pieces):
    return pl.pallas_call(
        stack_kernel,
        out_shape=jax.ShapeDtypeStruct((SHARDS, PIECE, HD), BF16),
        in_specs=[pl.BlockSpec(memory_space=pltpu.VMEM)],
        out_specs=pl.BlockSpec(memory_space=pltpu.VMEM),
        compiler_params=pltpu.CompilerParams(vmem_limit_bytes=8 * MIB),
        name="stack",
    )(pieces)


def segsum_kernel(flag_ref, in_ref, out_ref):
    total = jnp.zeros((PIECE, HD), F32)
    for t in range(SHARDS - 1, -1, -1):
        here = flag_ref[t].astype(F32) < MARK_MIN
        out_ref[t] = jnp.where(here, total, 0.0).astype(BF16)
        total = jnp.where(here, 0.0, total) + in_ref[t].astype(F32)


def segsum(flags, pieces):
    return pl.pallas_call(
        segsum_kernel,
        out_shape=jax.ShapeDtypeStruct((SHARDS, PIECE, HD), BF16),
        in_specs=[pl.BlockSpec(memory_space=pltpu.VMEM)] * 2,
        out_specs=pl.BlockSpec(memory_space=pltpu.VMEM),
        compiler_params=pltpu.CompilerParams(vmem_limit_bytes=8 * MIB),
        name="segsum",
    )(flags, pieces)


def final_kernel(count_ref, dk_ref, dv_ref, in_ref, gk_ref, gv_ref, acc):
    for half, (ref, out, scale) in enumerate(((dk_ref, gk_ref, SCALE), (dv_ref, gv_ref, 1.0))):
        acc[...] = ref[...]
        piece = in_ref[pl.ds(half * 16, 16)].astype(F32)
        for j in range(MAXA):
            last = last_of_depth(count_ref, j)
            row = pl.multiple_of(jnp.maximum(last, 0) * BLK, BLK)
            term = piece[:, 8 * j : 8 * j + 8, :].reshape(BLK, HD)
            acc[pl.ds(row, BLK), :] += jnp.where(last >= 0, term, 0.0)
        out[...] = (acc[...] * scale).astype(BF16)


def final(count, dk, dv, pieces):
    shape = jax.ShapeDtypeStruct((OWN * BLK, HD), BF16)
    return pl.pallas_call(
        final_kernel,
        out_shape=(shape, shape),
        in_specs=[pl.BlockSpec(memory_space=pltpu.SMEM)] + [pl.BlockSpec(memory_space=pltpu.VMEM)] * 3,
        out_specs=[pl.BlockSpec(memory_space=pltpu.VMEM)] * 2,
        scratch_shapes=[pltpu.VMEM((OWN * BLK, HD), F32)],
        compiler_params=pltpu.CompilerParams(vmem_limit_bytes=8 * MIB),
        name="final",
    )(count, dk, dv, pieces)


def nt(a, b):
    return lax.dot_general(a, b, (((1,), (1,)), ((), ())), preferred_element_type=F32)


def nn(a, b):
    return lax.dot_general(a, b, (((1,), (0,)), ((), ())), preferred_element_type=F32)


def tn(a, b):
    return lax.dot_general(a, b, (((0,), (0,)), ((), ())), preferred_element_type=F32)


def table_place(ids_ref, base, b, j):
    ident = ids_ref[b, j]
    place = jnp.where(ident >= base, ident - base, OWN + j)
    return pl.multiple_of(place * BLK, BLK)


def attn_kernel(
    ids_ref,
    count_ref,
    q_ref,
    o_ref,
    k_ref,
    v_ref,
    ext_ref,
    ds_ref,
    kt,
    dk_ref,
    dv_ref,
    back_ref,
    vt,
    dke,
    dve,
    kb,
    vb,
    dka,
    dva,
    *slots,
):
    b = pl.program_id(0)
    base = lax.axis_index("ctx") * OWN

    @pl.when(b == 0)
    def _():
        kt[pl.ds(0, OWN * BLK), :] = k_ref[...]
        vt[pl.ds(0, OWN * BLK), :] = v_ref[...]
        for half, tab in enumerate((kt, vt)):
            piece = ext_ref[pl.ds(half * 16, 16)].astype(F32)
            for j in range(MAXA):
                rows = piece[:, 8 * j : 8 * j + 8, :].reshape(BLK, HD)
                tab[pl.ds((OWN + j) * BLK, BLK), :] = rows.astype(BF16)
        dke[...] = jnp.zeros_like(dke)
        dve[...] = jnp.zeros_like(dve)

    count = count_ref[b]
    coef = SCALE * LOG2E
    heads = CHUNK // HD
    key_pos = lax.broadcasted_iota(jnp.int32, (BLK, CHUNK), 0)
    row_pos = lax.rem(lax.broadcasted_iota(jnp.int32, (BLK, CHUNK), 1), BLK)
    causal = key_pos <= row_pos

    def table_row(j):
        return table_place(ids_ref, base, b, j)

    def rows_of(ref, c):
        return jnp.concatenate(
            [ref[:, c * CHUNK + h * HD : c * CHUNK + (h + 1) * HD] for h in range(heads)], axis=0
        )

    def slot(c):
        return slots[3 * (c % 2) : 3 * (c % 2) + 3]

    def scores(n, c):
        nk = (n + 1) * BLK
        return nt(kb[pl.ds(0, nk), :], rows_of(q_ref, c)), nt(vb[pl.ds(0, nk), :], rows_of(o_ref, c))

    def keep(n, c, j, both):
        e_scr, d_scr, _ = slot(c)
        s, d = (x[j * BLK : (j + 1) * BLK] for x in both)
        if j == n:
            s = jnp.where(causal, s, -jnp.inf)
        top = jnp.max(s, axis=0, keepdims=True)
        e = jnp.exp2((s - top) * coef)
        e_scr[pl.ds(j * BLK, BLK), :] = e
        d_scr[pl.ds(j * BLK, BLK), :] = d
        return top, jnp.sum(e, axis=0, keepdims=True), jnp.sum(e * d, axis=0, keepdims=True)

    def merge(c, stats):
        g_scr = slot(c)[2]
        top = functools.reduce(jnp.maximum, [t for t, _, _ in stats])
        factors = [jnp.exp2((t - top) * coef) for t, _, _ in stats]
        inv = 1.0 / sum(f * x for f, (_, x, _) in zip(factors, stats))
        delta = sum(f * x for f, (_, _, x) in zip(factors, stats)) * inv
        for j, f in enumerate(factors):
            g_scr[j : j + 1, :] = f * inv
        g_scr[MAXA + 1 : MAXA + 2, :] = delta

    def weigh(c, j):
        e_scr, d_scr, g_scr = slot(c)
        p = e_scr[pl.ds(j * BLK, BLK), :] * g_scr[j : j + 1, :]
        ds = p * (d_scr[pl.ds(j * BLK, BLK), :] - g_scr[MAXA + 1 : MAXA + 2, :])
        ds = ds.astype(BF16)
        ds_ref[0, pl.ds(j * BLK, BLK), c * CHUNK : (c + 1) * CHUNK] = ds
        return p.astype(BF16), ds

    def add(n, c, tiles):
        nk = (n + 1) * BLK
        dv = nn(jnp.concatenate([p for p, _ in tiles], axis=0), rows_of(o_ref, c))
        dk = nn(jnp.concatenate([ds for _, ds in tiles], axis=0), rows_of(q_ref, c))
        if c == 0:
            dva[pl.ds(0, nk), :] = dv
            dka[pl.ds(0, nk), :] = dk
        else:
            dva[pl.ds(0, nk), :] += dv
            dka[pl.ds(0, nk), :] += dk

    for n in range(MAXA + 1):

        @pl.when(count == n)
        def _(n=n):
            places = [table_row(j) for j in range(n)] + [pl.multiple_of(b * BLK, BLK)]
            for j in range(n + 1):
                kb[pl.ds(j * BLK, BLK), :] = kt[pl.ds(places[j], BLK), :]
                vb[pl.ds(j * BLK, BLK), :] = vt[pl.ds(places[j], BLK), :]
            chunks = ROWS // CHUNK
            both = scores(n, 0)
            merge(0, [keep(n, 0, j, both) for j in range(n + 1)])
            for c in range(chunks):
                more = c + 1 < chunks
                if more:
                    both = scores(n, c + 1)
                tiles, stats = [], []
                for j in range(n + 1):
                    tiles.append(weigh(c, j))
                    if more:
                        stats.append(keep(n, c + 1, j, both))
                add(n, c, tiles)
                if more:
                    merge(c + 1, stats)
            for j in range(n + 1):
                dke[pl.ds(places[j], BLK), :] += dka[pl.ds(j * BLK, BLK), :]
                dve[pl.ds(places[j], BLK), :] += dva[pl.ds(j * BLK, BLK), :]

    @pl.when(b == OWN - 1)
    def _():
        dk_ref[...] = dke[pl.ds(0, OWN * BLK), :]
        dv_ref[...] = dve[pl.ds(0, OWN * BLK), :]
        for half, acc in enumerate((dke, dve)):
            parts = [acc[pl.ds((OWN + j) * BLK, BLK), :].reshape(16, 8, HD) for j in range(MAXA)]
            back_ref[pl.ds(half * 16, 16)] = jnp.concatenate(parts, axis=1).astype(BF16)


def attention(ids, count, queries, grad_out, keys, values, ext):
    whole = lambda shape: pl.BlockSpec(shape, lambda b, *_: (0,) * len(shape))
    tiles = OWN + MAXA
    return pl.pallas_call(
        attn_kernel,
        grid_spec=pltpu.PrefetchScalarGridSpec(
            num_scalar_prefetch=2,
            grid=(OWN,),
            in_specs=[
                pl.BlockSpec((BLK, ROWS), lambda b, *_: (b, 0)),
                pl.BlockSpec((BLK, ROWS), lambda b, *_: (b, 0)),
                whole((OWN * BLK, HD)),
                whole((OWN * BLK, HD)),
                whole((SHARDS, PIECE, HD)),
            ],
            out_specs=[
                pl.BlockSpec((1, (MAXA + 1) * BLK, ROWS), lambda b, *_: (b, 0, 0)),
                whole((tiles * BLK, HD)),
                whole((OWN * BLK, HD)),
                whole((OWN * BLK, HD)),
                whole((SHARDS, PIECE, HD)),
            ],
            scratch_shapes=[
                pltpu.VMEM((tiles * BLK, HD), BF16),
                pltpu.VMEM((tiles * BLK, HD), F32),
                pltpu.VMEM((tiles * BLK, HD), F32),
                pltpu.VMEM(((MAXA + 1) * BLK, HD), BF16),
                pltpu.VMEM(((MAXA + 1) * BLK, HD), BF16),
                pltpu.VMEM(((MAXA + 1) * BLK, HD), F32),
                pltpu.VMEM(((MAXA + 1) * BLK, HD), F32),
            ]
            + [
                pltpu.VMEM(((MAXA + 1) * BLK, CHUNK), F32),
                pltpu.VMEM(((MAXA + 1) * BLK, CHUNK), F32),
                pltpu.VMEM((8, CHUNK), F32),
            ]
            * 2,
        ),
        out_shape=(
            jax.ShapeDtypeStruct((OWN, (MAXA + 1) * BLK, ROWS), BF16),
            jax.ShapeDtypeStruct((tiles * BLK, HD), BF16),
            jax.ShapeDtypeStruct((OWN * BLK, HD), F32),
            jax.ShapeDtypeStruct((OWN * BLK, HD), F32),
            jax.ShapeDtypeStruct((SHARDS, PIECE, HD), BF16),
        ),
        compiler_params=pltpu.CompilerParams(vmem_limit_bytes=VMEM_A),
        name="attention",
    )(ids, count, queries, grad_out, keys, values, ext)


def query_kernel(ids_ref, count_ref, ds_ref, kt_ref, dq_ref, kb):
    b = pl.program_id(0)
    base = lax.axis_index("ctx") * OWN
    count = count_ref[b]
    for n in range(MAXA + 1):

        @pl.when(count == n)
        def _(n=n):
            places = [table_place(ids_ref, base, b, j) for j in range(n)]
            places.append(pl.multiple_of(b * BLK, BLK))
            for j in range(n + 1):
                kb[pl.ds(j * BLK, BLK), :] = kt_ref[pl.ds(places[j], BLK), :]
            nk = (n + 1) * BLK
            g = (tn(kb[pl.ds(0, nk), :], ds_ref[0, pl.ds(0, nk), :]) * SCALE).astype(BF16)
            for h in range(HQ):
                head = slice(h * HD, (h + 1) * HD)
                dq_ref[:, head] = g[:, head].T


def query_grads(ids, count, dscores, table):
    return pl.pallas_call(
        query_kernel,
        grid_spec=pltpu.PrefetchScalarGridSpec(
            num_scalar_prefetch=2,
            grid=(OWN,),
            in_specs=[
                pl.BlockSpec((1, (MAXA + 1) * BLK, ROWS), lambda b, *_: (b, 0, 0)),
                pl.BlockSpec(table.shape, lambda b, *_: (0, 0)),
            ],
            out_specs=pl.BlockSpec((BLK, ROWS), lambda b, *_: (b, 0)),
            scratch_shapes=[pltpu.VMEM(((MAXA + 1) * BLK, HD), BF16)],
        ),
        out_shape=jax.ShapeDtypeStruct((OWN * BLK, ROWS), BF16),
        compiler_params=pltpu.CompilerParams(vmem_limit_bytes=VMEM_Q),
        cost_estimate=pl.CostEstimate(
            flops=int(1e10), bytes_accessed=16 * MIB, transcendentals=0
        ),
        name="query_grads",
    )(ids, count, dscores, table)


def body(queries, keys, values, grad_out, ancestor_ids, ancestor_count):
    mine = pack(keys, values, ancestor_count)
    pieces = lax.all_to_all(mine, "ctx", 0, 0, tiled=True)
    ext = lax.all_to_all(stack(pieces), "ctx", 0, 0, tiled=True)
    scalars = (ancestor_ids, ancestor_count)
    dscores, table, dk, dv, back = attention(*scalars, queries, grad_out, keys, values, ext)
    grad_queries = query_grads(*scalars, dscores, table)
    got = lax.all_to_all(back, "ctx", 0, 0, tiled=True)
    got, grad_queries = lax.optimization_barrier((got, grad_queries))
    sums = segsum(pieces, got)
    terms = lax.all_to_all(sums, "ctx", 0, 0, tiled=True)
    grad_keys, grad_values = final(ancestor_count, dk, dv, terms)
    return (grad_queries, grad_keys, grad_values)


def solution(mesh):
    rows = P(("rep", "ctx"), "head")
    in_specs = (rows, rows, rows, rows, P(("rep", "ctx"), None), P(("rep", "ctx")))
    return jax.shard_map(
        body, mesh=mesh, in_specs=in_specs, out_specs=(rows, rows, rows), check_vma=False
    )
```

```python
import functools

import jax
import jax.numpy as jnp
from jax import lax
from jax.experimental import pallas as pl
from jax.experimental.pallas import tpu as pltpu
from jax.sharding import PartitionSpec as P

HD = 128
HQ = 8
BLK = 128
MAXA = 6
OWN = 8
SHARDS = 32
ROWS = HQ * BLK
CHUNK = 512
PIECE = 8 * MAXA
MARK = 1e30
MARK_MIN = 1e29
SCALE = HD ** (-0.5)
LOG2E = 1.4426950408889634
MIB = 1024 * 1024
VMEM_A = 50 * MIB
VMEM_Q = 40 * MIB

F32 = jnp.float32
BF16 = jnp.bfloat16


def last_of_depth(count_ref, depth):
    found = jnp.int32(-1)
    for b in range(OWN):
        found = jnp.where(count_ref[b] == depth, jnp.int32(b), found)
    return found


def pack_kernel(count_ref, k_ref, v_ref, out_ref):
    for half, ref in enumerate((k_ref, v_ref)):
        parts = []
        for j in range(MAXA):
            last = last_of_depth(count_ref, j)
            row = pl.multiple_of(jnp.maximum(last, 0) * BLK, BLK)
            block = ref[pl.ds(row, BLK), :].astype(F32)
            block = jnp.where(last >= 0, block, MARK)
            parts.append(block.reshape(16, 8, HD))
        out_ref[pl.ds(half * 16, 16)] = jnp.concatenate(parts, axis=1).astype(BF16)


def pack(keys, values, count):
    return pl.pallas_call(
        pack_kernel,
        out_shape=jax.ShapeDtypeStruct((SHARDS, PIECE, HD), BF16),
        in_specs=[
            pl.BlockSpec(memory_space=pltpu.SMEM),
            pl.BlockSpec(memory_space=pltpu.VMEM),
            pl.BlockSpec(memory_space=pltpu.VMEM),
        ],
        out_specs=pl.BlockSpec(memory_space=pltpu.VMEM),
        name="pack",
    )(count, keys, values)


def stack_kernel(in_ref, out_ref):
    held = jnp.full((PIECE, HD), MARK, F32)
    for t in range(SHARDS):
        out_ref[t] = held.astype(BF16)
        x = in_ref[t].astype(F32)
        held = jnp.where(x < MARK_MIN, x, held)


def stack(pieces):
    return pl.pallas_call(
        stack_kernel,
        out_shape=jax.ShapeDtypeStruct((SHARDS, PIECE, HD), BF16),
        in_specs=[pl.BlockSpec(memory_space=pltpu.VMEM)],
        out_specs=pl.BlockSpec(memory_space=pltpu.VMEM),
        compiler_params=pltpu.CompilerParams(vmem_limit_bytes=8 * MIB),
        name="stack",
    )(pieces)


def segsum_kernel(flag_ref, in_ref, out_ref):
    total = jnp.zeros((PIECE, HD), F32)
    for t in range(SHARDS - 1, -1, -1):
        here = flag_ref[t].astype(F32) < MARK_MIN
        out_ref[t] = jnp.where(here, total, 0.0).astype(BF16)
        total = jnp.where(here, 0.0, total) + in_ref[t].astype(F32)


def segsum(flags, pieces):
    return pl.pallas_call(
        segsum_kernel,
        out_shape=jax.ShapeDtypeStruct((SHARDS, PIECE, HD), BF16),
        in_specs=[pl.BlockSpec(memory_space=pltpu.VMEM)] * 2,
        out_specs=pl.BlockSpec(memory_space=pltpu.VMEM),
        compiler_params=pltpu.CompilerParams(vmem_limit_bytes=8 * MIB),
        name="segsum",
    )(flags, pieces)


def final_kernel(count_ref, dk_ref, dv_ref, in_ref, gk_ref, gv_ref, acc):
    for half, (ref, out, scale) in enumerate(((dk_ref, gk_ref, SCALE), (dv_ref, gv_ref, 1.0))):
        acc[...] = ref[...]
        piece = in_ref[pl.ds(half * 16, 16)].astype(F32)
        for j in range(MAXA):
            last = last_of_depth(count_ref, j)
            row = pl.multiple_of(jnp.maximum(last, 0) * BLK, BLK)
            term = piece[:, 8 * j : 8 * j + 8, :].reshape(BLK, HD)
            acc[pl.ds(row, BLK), :] += jnp.where(last >= 0, term, 0.0)
        out[...] = (acc[...] * scale).astype(BF16)


def final(count, dk, dv, pieces):
    shape = jax.ShapeDtypeStruct((OWN * BLK, HD), BF16)
    return pl.pallas_call(
        final_kernel,
        out_shape=(shape, shape),
        in_specs=[pl.BlockSpec(memory_space=pltpu.SMEM)] + [pl.BlockSpec(memory_space=pltpu.VMEM)] * 3,
        out_specs=[pl.BlockSpec(memory_space=pltpu.VMEM)] * 2,
        scratch_shapes=[pltpu.VMEM((OWN * BLK, HD), F32)],
        compiler_params=pltpu.CompilerParams(vmem_limit_bytes=8 * MIB),
        name="final",
    )(count, dk, dv, pieces)


def nt(a, b):
    return lax.dot_general(a, b, (((1,), (1,)), ((), ())), preferred_element_type=F32)


def nn(a, b):
    return lax.dot_general(a, b, (((1,), (0,)), ((), ())), preferred_element_type=F32)


def tn(a, b):
    return lax.dot_general(a, b, (((0,), (0,)), ((), ())), preferred_element_type=F32)


def table_place(ids_ref, base, b, j):
    ident = ids_ref[b, j]
    place = jnp.where(ident >= base, ident - base, OWN + j)
    return pl.multiple_of(place * BLK, BLK)


def attn_kernel(
    ids_ref,
    count_ref,
    q_ref,
    o_ref,
    k_ref,
    v_ref,
    ext_ref,
    ds_ref,
    kt,
    dk_ref,
    dv_ref,
    back_ref,
    vt,
    dke,
    dve,
    kb,
    vb,
    dka,
    dva,
    *slots,
):
    b = pl.program_id(0)
    base = lax.axis_index("ctx") * OWN

    @pl.when(b == 0)
    def _():
        kt[pl.ds(0, OWN * BLK), :] = k_ref[...]
        vt[pl.ds(0, OWN * BLK), :] = v_ref[...]
        for half, tab in enumerate((kt, vt)):
            piece = ext_ref[pl.ds(half * 16, 16)].astype(F32)
            for j in range(MAXA):
                rows = piece[:, 8 * j : 8 * j + 8, :].reshape(BLK, HD)
                tab[pl.ds((OWN + j) * BLK, BLK), :] = rows.astype(BF16)
        dke[...] = jnp.zeros_like(dke)
        dve[...] = jnp.zeros_like(dve)

    count = count_ref[b]
    coef = SCALE * LOG2E
    heads = CHUNK // HD
    key_pos = lax.broadcasted_iota(jnp.int32, (BLK, CHUNK), 0)
    row_pos = lax.rem(lax.broadcasted_iota(jnp.int32, (BLK, CHUNK), 1), BLK)
    causal = key_pos <= row_pos

    def table_row(j):
        return table_place(ids_ref, base, b, j)

    def rows_of(ref, c):
        return jnp.concatenate(
            [ref[:, c * CHUNK + h * HD : c * CHUNK + (h + 1) * HD] for h in range(heads)], axis=0
        )

    def slot(c):
        return slots[3 * (c % 2) : 3 * (c % 2) + 3]

    def scores(n, c):
        nk = (n + 1) * BLK
        return nt(kb[pl.ds(0, nk), :], rows_of(q_ref, c)), nt(vb[pl.ds(0, nk), :], rows_of(o_ref, c))

    def keep(n, c, j, both):
        e_scr, d_scr, _ = slot(c)
        s, d = (x[j * BLK : (j + 1) * BLK] for x in both)
        if j == n:
            s = jnp.where(causal, s, -jnp.inf)
        top = jnp.max(s, axis=0, keepdims=True)
        e = jnp.exp2((s - top) * coef)
        e_scr[pl.ds(j * BLK, BLK), :] = e
        d_scr[pl.ds(j * BLK, BLK), :] = d
        return top, jnp.sum(e, axis=0, keepdims=True), jnp.sum(e * d, axis=0, keepdims=True)

    def merge(c, stats):
        g_scr = slot(c)[2]
        top = functools.reduce(jnp.maximum, [t for t, _, _ in stats])
        factors = [jnp.exp2((t - top) * coef) for t, _, _ in stats]
        inv = 1.0 / sum(f * x for f, (_, x, _) in zip(factors, stats))
        delta = sum(f * x for f, (_, _, x) in zip(factors, stats)) * inv
        for j, f in enumerate(factors):
            g_scr[j : j + 1, :] = f * inv
        g_scr[MAXA + 1 : MAXA + 2, :] = delta

    def weigh(c, j):
        e_scr, d_scr, g_scr = slot(c)
        p = e_scr[pl.ds(j * BLK, BLK), :] * g_scr[j : j + 1, :]
        ds = p * (d_scr[pl.ds(j * BLK, BLK), :] - g_scr[MAXA + 1 : MAXA + 2, :])
        ds = ds.astype(BF16)
        ds_ref[0, pl.ds(j * BLK, BLK), c * CHUNK : (c + 1) * CHUNK] = ds
        return p.astype(BF16), ds

    def add(n, c, tiles):
        nk = (n + 1) * BLK
        dv = nn(jnp.concatenate([p for p, _ in tiles], axis=0), rows_of(o_ref, c))
        dk = nn(jnp.concatenate([ds for _, ds in tiles], axis=0), rows_of(q_ref, c))
        if c == 0:
            dva[pl.ds(0, nk), :] = dv
            dka[pl.ds(0, nk), :] = dk
        else:
            dva[pl.ds(0, nk), :] += dv
            dka[pl.ds(0, nk), :] += dk

    for n in range(MAXA + 1):

        @pl.when(count == n)
        def _(n=n):
            places = [table_row(j) for j in range(n)] + [pl.multiple_of(b * BLK, BLK)]
            for j in range(n + 1):
                kb[pl.ds(j * BLK, BLK), :] = kt[pl.ds(places[j], BLK), :]
                vb[pl.ds(j * BLK, BLK), :] = vt[pl.ds(places[j], BLK), :]
            chunks = ROWS // CHUNK
            both = scores(n, 0)
            merge(0, [keep(n, 0, j, both) for j in range(n + 1)])
            for c in range(chunks):
                more = c + 1 < chunks
                if more:
                    both = scores(n, c + 1)
                tiles, stats = [], []
                for j in range(n + 1):
                    tiles.append(weigh(c, j))
                    if more:
                        stats.append(keep(n, c + 1, j, both))
                add(n, c, tiles)
                if more:
                    merge(c + 1, stats)
            for j in range(n + 1):
                dke[pl.ds(places[j], BLK), :] += dka[pl.ds(j * BLK, BLK), :]
                dve[pl.ds(places[j], BLK), :] += dva[pl.ds(j * BLK, BLK), :]

    @pl.when(b == OWN - 1)
    def _():
        dk_ref[...] = dke[pl.ds(0, OWN * BLK), :]
        dv_ref[...] = dve[pl.ds(0, OWN * BLK), :]
        for half, acc in enumerate((dke, dve)):
            parts = [acc[pl.ds((OWN + j) * BLK, BLK), :].reshape(16, 8, HD) for j in range(MAXA)]
            back_ref[pl.ds(half * 16, 16)] = jnp.concatenate(parts, axis=1).astype(BF16)


def attention(ids, count, queries, grad_out, keys, values, ext):
    whole = lambda shape: pl.BlockSpec(shape, lambda b, *_: (0,) * len(shape))
    tiles = OWN + MAXA
    return pl.pallas_call(
        attn_kernel,
        grid_spec=pltpu.PrefetchScalarGridSpec(
            num_scalar_prefetch=2,
            grid=(OWN,),
            in_specs=[
                pl.BlockSpec((BLK, ROWS), lambda b, *_: (b, 0)),
                pl.BlockSpec((BLK, ROWS), lambda b, *_: (b, 0)),
                whole((OWN * BLK, HD)),
                whole((OWN * BLK, HD)),
                whole((SHARDS, PIECE, HD)),
            ],
            out_specs=[
                pl.BlockSpec((1, (MAXA + 1) * BLK, ROWS), lambda b, *_: (b, 0, 0)),
                whole((tiles * BLK, HD)),
                whole((OWN * BLK, HD)),
                whole((OWN * BLK, HD)),
                whole((SHARDS, PIECE, HD)),
            ],
            scratch_shapes=[
                pltpu.VMEM((tiles * BLK, HD), BF16),
                pltpu.VMEM((tiles * BLK, HD), F32),
                pltpu.VMEM((tiles * BLK, HD), F32),
                pltpu.VMEM(((MAXA + 1) * BLK, HD), BF16),
                pltpu.VMEM(((MAXA + 1) * BLK, HD), BF16),
                pltpu.VMEM(((MAXA + 1) * BLK, HD), F32),
                pltpu.VMEM(((MAXA + 1) * BLK, HD), F32),
            ]
            + [
                pltpu.VMEM(((MAXA + 1) * BLK, CHUNK), F32),
                pltpu.VMEM(((MAXA + 1) * BLK, CHUNK), F32),
                pltpu.VMEM((8, CHUNK), F32),
            ]
            * 2,
        ),
        out_shape=(
            jax.ShapeDtypeStruct((OWN, (MAXA + 1) * BLK, ROWS), BF16),
            jax.ShapeDtypeStruct((tiles * BLK, HD), BF16),
            jax.ShapeDtypeStruct((OWN * BLK, HD), F32),
            jax.ShapeDtypeStruct((OWN * BLK, HD), F32),
            jax.ShapeDtypeStruct((SHARDS, PIECE, HD), BF16),
        ),
        compiler_params=pltpu.CompilerParams(vmem_limit_bytes=VMEM_A),
        name="attention",
    )(ids, count, queries, grad_out, keys, values, ext)


def query_kernel(ids_ref, count_ref, ds_ref, kt_ref, dq_ref, kb, held, sems):
    b = pl.program_id(0)
    base = lax.axis_index("ctx") * OWN

    def fetch(block, j):
        rows = pl.ds(j * BLK, BLK)
        return pltpu.make_async_copy(
            ds_ref.at[block, rows, :], held.at[block, rows, :], sems.at[block, j]
        )

    @pl.when(b == 0)
    def _():
        for block in range(OWN):
            for j in range(MAXA + 1):

                @pl.when(j <= count_ref[block])
                def _(block=block, j=j):
                    fetch(block, j).start()

    count = count_ref[b]
    for n in range(MAXA + 1):

        @pl.when(count == n)
        def _(n=n):
            places = [table_place(ids_ref, base, b, j) for j in range(n)]
            places.append(pl.multiple_of(b * BLK, BLK))
            for j in range(n + 1):
                kb[pl.ds(j * BLK, BLK), :] = kt_ref[pl.ds(places[j], BLK), :]
            for j in range(n + 1):
                fetch(b, j).wait()
            nk = (n + 1) * BLK
            g = (tn(kb[pl.ds(0, nk), :], held[b, pl.ds(0, nk), :]) * SCALE).astype(BF16)
            for h in range(HQ):
                head = slice(h * HD, (h + 1) * HD)
                dq_ref[:, head] = g[:, head].T


def query_grads(ids, count, dscores, table):
    return pl.pallas_call(
        query_kernel,
        grid_spec=pltpu.PrefetchScalarGridSpec(
            num_scalar_prefetch=2,
            grid=(OWN,),
            in_specs=[
                pl.BlockSpec(memory_space=pl.ANY),
                pl.BlockSpec(table.shape, lambda b, *_: (0, 0)),
            ],
            out_specs=pl.BlockSpec((BLK, ROWS), lambda b, *_: (b, 0)),
            scratch_shapes=[
                pltpu.VMEM(((MAXA + 1) * BLK, HD), BF16),
                pltpu.VMEM((OWN, (MAXA + 1) * BLK, ROWS), BF16),
                pltpu.SemaphoreType.DMA((OWN, MAXA + 1)),
            ],
        ),
        out_shape=jax.ShapeDtypeStruct((OWN * BLK, ROWS), BF16),
        compiler_params=pltpu.CompilerParams(vmem_limit_bytes=VMEM_Q),
        cost_estimate=pl.CostEstimate(
            flops=int(1e10), bytes_accessed=16 * MIB, transcendentals=0
        ),
        name="query_grads",
    )(ids, count, dscores, table)


def body(queries, keys, values, grad_out, ancestor_ids, ancestor_count):
    mine = pack(keys, values, ancestor_count)
    pieces = lax.all_to_all(mine, "ctx", 0, 0, tiled=True)
    ext = lax.all_to_all(stack(pieces), "ctx", 0, 0, tiled=True)
    scalars = (ancestor_ids, ancestor_count)
    dscores, table, dk, dv, back = attention(*scalars, queries, grad_out, keys, values, ext)
    grad_queries = query_grads(*scalars, dscores, table)
    sums = segsum(pieces, lax.all_to_all(back, "ctx", 0, 0, tiled=True))
    terms = lax.all_to_all(sums, "ctx", 0, 0, tiled=True)
    grad_keys, grad_values = final(ancestor_count, dk, dv, terms)
    return (grad_queries, grad_keys, grad_values)


def solution(mesh):
    rows = P(("rep", "ctx"), "head")
    in_specs = (rows, rows, rows, rows, P(("rep", "ctx"), None), P(("rep", "ctx")))
    return jax.shard_map(
        body, mesh=mesh, in_specs=in_specs, out_specs=(rows, rows, rows), check_vma=False
    )
```

```python
import functools

import jax
import jax.numpy as jnp
from jax import lax
from jax.experimental import pallas as pl
from jax.experimental.pallas import tpu as pltpu
from jax.sharding import PartitionSpec as P

HD = 128
HQ = 8
BLK = 128
MAXA = 6
OWN = 8
SHARDS = 32
ROWS = HQ * BLK
CHUNK = 512
PAIR = 2
PIECE = 8 * MAXA
MARK = 1e30
MARK_MIN = 1e29
SCALE = HD ** (-0.5)
LOG2E = 1.4426950408889634
MIB = 1024 * 1024
VMEM_A = 50 * MIB
VMEM_Q = 40 * MIB

F32 = jnp.float32
BF16 = jnp.bfloat16


def last_of_depth(count_ref, depth):
    found = jnp.int32(-1)
    for b in range(OWN):
        found = jnp.where(count_ref[b] == depth, jnp.int32(b), found)
    return found


def pack_kernel(count_ref, k_ref, v_ref, out_ref):
    for half, ref in enumerate((k_ref, v_ref)):
        parts = []
        for j in range(MAXA):
            last = last_of_depth(count_ref, j)
            row = pl.multiple_of(jnp.maximum(last, 0) * BLK, BLK)
            block = ref[pl.ds(row, BLK), :].astype(F32)
            block = jnp.where(last >= 0, block, MARK)
            parts.append(block.reshape(16, 8, HD))
        out_ref[pl.ds(half * 16, 16)] = jnp.concatenate(parts, axis=1).astype(BF16)


def pack(keys, values, count):
    return pl.pallas_call(
        pack_kernel,
        out_shape=jax.ShapeDtypeStruct((SHARDS, PIECE, HD), BF16),
        in_specs=[
            pl.BlockSpec(memory_space=pltpu.SMEM),
            pl.BlockSpec(memory_space=pltpu.VMEM),
            pl.BlockSpec(memory_space=pltpu.VMEM),
        ],
        out_specs=pl.BlockSpec(memory_space=pltpu.VMEM),
        name="pack",
    )(count, keys, values)


def stack_kernel(in_ref, out_ref):
    held = jnp.full((PIECE, HD), MARK, F32)
    for t in range(SHARDS):
        out_ref[t] = held.astype(BF16)
        x = in_ref[t].astype(F32)
        held = jnp.where(x < MARK_MIN, x, held)


def stack(pieces):
    return pl.pallas_call(
        stack_kernel,
        out_shape=jax.ShapeDtypeStruct((SHARDS, PIECE, HD), BF16),
        in_specs=[pl.BlockSpec(memory_space=pltpu.VMEM)],
        out_specs=pl.BlockSpec(memory_space=pltpu.VMEM),
        compiler_params=pltpu.CompilerParams(vmem_limit_bytes=8 * MIB),
        name="stack",
    )(pieces)


def segsum_kernel(flag_ref, in_ref, out_ref):
    total = jnp.zeros((PIECE, HD), F32)
    for t in range(SHARDS - 1, -1, -1):
        here = flag_ref[t].astype(F32) < MARK_MIN
        out_ref[t] = jnp.where(here, total, 0.0).astype(BF16)
        total = jnp.where(here, 0.0, total) + in_ref[t].astype(F32)


def segsum(flags, pieces):
    return pl.pallas_call(
        segsum_kernel,
        out_shape=jax.ShapeDtypeStruct((SHARDS, PIECE, HD), BF16),
        in_specs=[pl.BlockSpec(memory_space=pltpu.VMEM)] * 2,
        out_specs=pl.BlockSpec(memory_space=pltpu.VMEM),
        compiler_params=pltpu.CompilerParams(vmem_limit_bytes=8 * MIB),
        name="segsum",
    )(flags, pieces)


def final_kernel(count_ref, dk_ref, dv_ref, in_ref, gk_ref, gv_ref, acc):
    for half, (ref, out, scale) in enumerate(((dk_ref, gk_ref, SCALE), (dv_ref, gv_ref, 1.0))):
        acc[...] = ref[...]
        piece = in_ref[pl.ds(half * 16, 16)].astype(F32)
        for j in range(MAXA):
            last = last_of_depth(count_ref, j)
            row = pl.multiple_of(jnp.maximum(last, 0) * BLK, BLK)
            term = piece[:, 8 * j : 8 * j + 8, :].reshape(BLK, HD)
            acc[pl.ds(row, BLK), :] += jnp.where(last >= 0, term, 0.0)
        out[...] = (acc[...] * scale).astype(BF16)


def final(count, dk, dv, pieces):
    shape = jax.ShapeDtypeStruct((OWN * BLK, HD), BF16)
    return pl.pallas_call(
        final_kernel,
        out_shape=(shape, shape),
        in_specs=[pl.BlockSpec(memory_space=pltpu.SMEM)] + [pl.BlockSpec(memory_space=pltpu.VMEM)] * 3,
        out_specs=[pl.BlockSpec(memory_space=pltpu.VMEM)] * 2,
        scratch_shapes=[pltpu.VMEM((OWN * BLK, HD), F32)],
        compiler_params=pltpu.CompilerParams(vmem_limit_bytes=8 * MIB),
        name="final",
    )(count, dk, dv, pieces)


def nt(a, b):
    return lax.dot_general(a, b, (((1,), (1,)), ((), ())), preferred_element_type=F32)


def nn(a, b):
    return lax.dot_general(a, b, (((1,), (0,)), ((), ())), preferred_element_type=F32)


def tn(a, b):
    return lax.dot_general(a, b, (((0,), (0,)), ((), ())), preferred_element_type=F32)


def table_place(ids_ref, base, b, j):
    ident = ids_ref[b, j]
    place = jnp.where(ident >= base, ident - base, OWN + j)
    return pl.multiple_of(place * BLK, BLK)


def attn_kernel(
    ids_ref,
    count_ref,
    q_ref,
    o_ref,
    k_ref,
    v_ref,
    ext_ref,
    ds_ref,
    kt,
    dk_ref,
    dv_ref,
    back_ref,
    vt,
    dke,
    dve,
    kb,
    vb,
    dka,
    dva,
    *slots,
):
    step = pl.program_id(0)
    base = lax.axis_index("ctx") * OWN

    @pl.when(step == 0)
    def _():
        kt[pl.ds(0, OWN * BLK), :] = k_ref[...]
        vt[pl.ds(0, OWN * BLK), :] = v_ref[...]
        for half, tab in enumerate((kt, vt)):
            piece = ext_ref[pl.ds(half * 16, 16)].astype(F32)
            for j in range(MAXA):
                rows = piece[:, 8 * j : 8 * j + 8, :].reshape(BLK, HD)
                rows = jnp.where(rows < MARK_MIN, rows, 0.0)
                tab[pl.ds((OWN + j) * BLK, BLK), :] = rows.astype(BF16)
        dke[...] = jnp.zeros_like(dke)
        dve[...] = jnp.zeros_like(dve)

    counts = [count_ref[step * PAIR + i] for i in range(PAIR)]
    count = functools.reduce(jnp.maximum, counts)
    per_block = ROWS // CHUNK
    coef = SCALE * LOG2E
    heads = CHUNK // HD
    key_pos = lax.broadcasted_iota(jnp.int32, (BLK, CHUNK), 0)
    row_pos = lax.rem(lax.broadcasted_iota(jnp.int32, (BLK, CHUNK), 1), BLK)
    causal = key_pos <= row_pos

    def table_row(i, j):
        return table_place(ids_ref, base, step * PAIR + i, j)

    def rows_of(ref, c):
        block, c = divmod(c, per_block)
        rows = pl.ds(block * BLK, BLK)
        return jnp.concatenate(
            [ref[rows, c * CHUNK + h * HD : c * CHUNK + (h + 1) * HD] for h in range(heads)], axis=0
        )

    def slot(c):
        return slots[3 * (c % 2) : 3 * (c % 2) + 3]

    def scores(n, c):
        nk = (n + 1) * BLK
        block = c // per_block
        s = nt(kb[block, pl.ds(0, nk), :], rows_of(q_ref, c))
        return s, nt(vb[block, pl.ds(0, nk), :], rows_of(o_ref, c))

    def keep(n, c, j, both):
        e_scr, d_scr, _ = slot(c)
        s, d = (x[j * BLK : (j + 1) * BLK] for x in both)
        if j == n:
            s = jnp.where(causal, s, -jnp.inf)
        top = jnp.max(s, axis=0, keepdims=True)
        e = jnp.exp2((s - top) * coef)
        e_scr[pl.ds(j * BLK, BLK), :] = e
        d_scr[pl.ds(j * BLK, BLK), :] = d
        if j < n:
            top = jnp.where(j < counts[c // per_block], top, -MARK)
        return top, jnp.sum(e, axis=0, keepdims=True), jnp.sum(e * d, axis=0, keepdims=True)

    def merge(c, stats):
        g_scr = slot(c)[2]
        top = functools.reduce(jnp.maximum, [t for t, _, _ in stats])
        factors = [jnp.exp2((t - top) * coef) for t, _, _ in stats]
        inv = 1.0 / sum(f * x for f, (_, x, _) in zip(factors, stats))
        delta = sum(f * x for f, (_, _, x) in zip(factors, stats)) * inv
        for j, f in enumerate(factors):
            g_scr[j : j + 1, :] = f * inv
        g_scr[MAXA + 1 : MAXA + 2, :] = delta

    def weigh(n, c, j):
        e_scr, d_scr, g_scr = slot(c)
        p = e_scr[pl.ds(j * BLK, BLK), :] * g_scr[j : j + 1, :]
        ds = p * (d_scr[pl.ds(j * BLK, BLK), :] - g_scr[MAXA + 1 : MAXA + 2, :])
        ds = ds.astype(BF16)
        block, c = divmod(c, per_block)
        row = pl.multiple_of(counts[block] * BLK, BLK) if j == n else j * BLK
        ds_ref[block, pl.ds(row, BLK), c * CHUNK : (c + 1) * CHUNK] = ds
        return p.astype(BF16), ds

    def add(n, c, tiles):
        nk = (n + 1) * BLK
        dv = nn(jnp.concatenate([p for p, _ in tiles], axis=0), rows_of(o_ref, c))
        dk = nn(jnp.concatenate([ds for _, ds in tiles], axis=0), rows_of(q_ref, c))
        block, c = divmod(c, per_block)
        if c == 0:
            dva[block, pl.ds(0, nk), :] = dv
            dka[block, pl.ds(0, nk), :] = dk
        else:
            dva[block, pl.ds(0, nk), :] += dv
            dka[block, pl.ds(0, nk), :] += dk

    for n in range(MAXA + 1):

        @pl.when(count == n)
        def _(n=n):
            places = [
                [table_row(i, j) for j in range(n)]
                + [pl.multiple_of((step * PAIR + i) * BLK, BLK)]
                for i in range(PAIR)
            ]
            for i in range(PAIR):
                for j in range(n + 1):
                    kb[i, pl.ds(j * BLK, BLK), :] = kt[pl.ds(places[i][j], BLK), :]
                    vb[i, pl.ds(j * BLK, BLK), :] = vt[pl.ds(places[i][j], BLK), :]
            chunks = PAIR * per_block
            both = scores(n, 0)
            merge(0, [keep(n, 0, j, both) for j in range(n + 1)])
            for c in range(chunks):
                more = c + 1 < chunks
                if more:
                    both = scores(n, c + 1)
                tiles, stats = [], []
                for j in range(n + 1):
                    tiles.append(weigh(n, c, j))
                    if more:
                        stats.append(keep(n, c + 1, j, both))
                add(n, c, tiles)
                if more:
                    merge(c + 1, stats)
            for i in range(PAIR):
                for j in range(n + 1):
                    dke[pl.ds(places[i][j], BLK), :] += dka[i, pl.ds(j * BLK, BLK), :]
                    dve[pl.ds(places[i][j], BLK), :] += dva[i, pl.ds(j * BLK, BLK), :]

    @pl.when(step == OWN // PAIR - 1)
    def _():
        dk_ref[...] = dke[pl.ds(0, OWN * BLK), :]
        dv_ref[...] = dve[pl.ds(0, OWN * BLK), :]
        for half, acc in enumerate((dke, dve)):
            parts = [acc[pl.ds((OWN + j) * BLK, BLK), :].reshape(16, 8, HD) for j in range(MAXA)]
            back_ref[pl.ds(half * 16, 16)] = jnp.concatenate(parts, axis=1).astype(BF16)


def attention(ids, count, queries, grad_out, keys, values, ext):
    whole = lambda shape: pl.BlockSpec(shape, lambda b, *_: (0,) * len(shape))
    tiles = OWN + MAXA
    return pl.pallas_call(
        attn_kernel,
        grid_spec=pltpu.PrefetchScalarGridSpec(
            num_scalar_prefetch=2,
            grid=(OWN // PAIR,),
            in_specs=[
                pl.BlockSpec((PAIR * BLK, ROWS), lambda b, *_: (b, 0)),
                pl.BlockSpec((PAIR * BLK, ROWS), lambda b, *_: (b, 0)),
                whole((OWN * BLK, HD)),
                whole((OWN * BLK, HD)),
                whole((SHARDS, PIECE, HD)),
            ],
            out_specs=[
                pl.BlockSpec((PAIR, (MAXA + 1) * BLK, ROWS), lambda b, *_: (b, 0, 0)),
                whole((tiles * BLK, HD)),
                whole((OWN * BLK, HD)),
                whole((OWN * BLK, HD)),
                whole((SHARDS, PIECE, HD)),
            ],
            scratch_shapes=[
                pltpu.VMEM((tiles * BLK, HD), BF16),
                pltpu.VMEM((tiles * BLK, HD), F32),
                pltpu.VMEM((tiles * BLK, HD), F32),
                pltpu.VMEM((PAIR, (MAXA + 1) * BLK, HD), BF16),
                pltpu.VMEM((PAIR, (MAXA + 1) * BLK, HD), BF16),
                pltpu.VMEM((PAIR, (MAXA + 1) * BLK, HD), F32),
                pltpu.VMEM((PAIR, (MAXA + 1) * BLK, HD), F32),
            ]
            + [
                pltpu.VMEM(((MAXA + 1) * BLK, CHUNK), F32),
                pltpu.VMEM(((MAXA + 1) * BLK, CHUNK), F32),
                pltpu.VMEM((8, CHUNK), F32),
            ]
            * 2,
        ),
        out_shape=(
            jax.ShapeDtypeStruct((OWN, (MAXA + 1) * BLK, ROWS), BF16),
            jax.ShapeDtypeStruct((tiles * BLK, HD), BF16),
            jax.ShapeDtypeStruct((OWN * BLK, HD), F32),
            jax.ShapeDtypeStruct((OWN * BLK, HD), F32),
            jax.ShapeDtypeStruct((SHARDS, PIECE, HD), BF16),
        ),
        compiler_params=pltpu.CompilerParams(vmem_limit_bytes=VMEM_A),
        name="attention",
    )(ids, count, queries, grad_out, keys, values, ext)


def query_kernel(ids_ref, count_ref, ds_ref, kt_ref, dq_ref, kb, held, sems):
    b = pl.program_id(0)
    base = lax.axis_index("ctx") * OWN

    def fetch(block, j):
        rows = pl.ds(j * BLK, BLK)
        return pltpu.make_async_copy(
            ds_ref.at[block, rows, :], held.at[block, rows, :], sems.at[block, j]
        )

    @pl.when(b == 0)
    def _():
        for block in range(OWN):
            for j in range(MAXA + 1):

                @pl.when(j <= count_ref[block])
                def _(block=block, j=j):
                    fetch(block, j).start()

    count = count_ref[b]
    for n in range(MAXA + 1):

        @pl.when(count == n)
        def _(n=n):
            places = [table_place(ids_ref, base, b, j) for j in range(n)]
            places.append(pl.multiple_of(b * BLK, BLK))
            for j in range(n + 1):
                kb[pl.ds(j * BLK, BLK), :] = kt_ref[pl.ds(places[j], BLK), :]
            for j in range(n + 1):
                fetch(b, j).wait()
            nk = (n + 1) * BLK
            g = (tn(kb[pl.ds(0, nk), :], held[b, pl.ds(0, nk), :]) * SCALE).astype(BF16)
            for h in range(HQ):
                head = slice(h * HD, (h + 1) * HD)
                dq_ref[:, head] = g[:, head].T


def query_grads(ids, count, dscores, table):
    return pl.pallas_call(
        query_kernel,
        grid_spec=pltpu.PrefetchScalarGridSpec(
            num_scalar_prefetch=2,
            grid=(OWN,),
            in_specs=[
                pl.BlockSpec(memory_space=pl.ANY),
                pl.BlockSpec(table.shape, lambda b, *_: (0, 0)),
            ],
            out_specs=pl.BlockSpec((BLK, ROWS), lambda b, *_: (b, 0)),
            scratch_shapes=[
                pltpu.VMEM(((MAXA + 1) * BLK, HD), BF16),
                pltpu.VMEM((OWN, (MAXA + 1) * BLK, ROWS), BF16),
                pltpu.SemaphoreType.DMA((OWN, MAXA + 1)),
            ],
        ),
        out_shape=jax.ShapeDtypeStruct((OWN * BLK, ROWS), BF16),
        compiler_params=pltpu.CompilerParams(vmem_limit_bytes=VMEM_Q),
        cost_estimate=pl.CostEstimate(
            flops=int(1e10), bytes_accessed=16 * MIB, transcendentals=0
        ),
        name="query_grads",
    )(ids, count, dscores, table)


def body(queries, keys, values, grad_out, ancestor_ids, ancestor_count):
    mine = pack(keys, values, ancestor_count)
    pieces = lax.all_to_all(mine, "ctx", 0, 0, tiled=True)
    ext = lax.all_to_all(stack(pieces), "ctx", 0, 0, tiled=True)
    scalars = (ancestor_ids, ancestor_count)
    dscores, table, dk, dv, back = attention(*scalars, queries, grad_out, keys, values, ext)
    grad_queries = query_grads(*scalars, dscores, table)
    sums = segsum(pieces, lax.all_to_all(back, "ctx", 0, 0, tiled=True))
    terms = lax.all_to_all(sums, "ctx", 0, 0, tiled=True)
    grad_keys, grad_values = final(ancestor_count, dk, dv, terms)
    return (grad_queries, grad_keys, grad_values)


def solution(mesh):
    rows = P(("rep", "ctx"), "head")
    in_specs = (rows, rows, rows, rows, P(("rep", "ctx"), None), P(("rep", "ctx")))
    return jax.shard_map(
        body, mesh=mesh, in_specs=in_specs, out_specs=(rows, rows, rows), check_vma=False
    )
```
